32 devices in a mesh: dp: 4 (over x, core), mp: 8 (over z, y).
Axes of the slice: x: 2, y: 2, z: 4, core: 2. Of those that a mesh axis runs over, the one named last changes fastest.
Arguments:
- tokens: float32 [24576, 1024], P(('dp', 'mp')), may hold values from -12 to 12
- cotangent: float32 [24576, 1024], P(('dp', 'mp')), may hold values from -6 to 6
- group_items: int32 [4], P('dp'), may hold values from 1 to 3, as said below
- dataset_ids: int32 [12], P('dp'), may hold values from 0 to 4
- lead_hours: int32 [12], P('dp'), may hold values from 6 to 168
- set_weights: float32 [5], replicated, may hold values from 0.5 to 2
- lead_weight: float32 [1024], replicated, may hold values from -1.5 to 1.5
- lead_shift: float32 [1024], replicated, may hold values from -1 to 1
- norm_one_gain: float32 [1024], replicated, may hold values from 0.25 to 1.75
- norm_one_shift: float32 [1024], replicated, may hold values from -0.9 to 0.9
- heads_weight: bfloat16 [1024, 3072], P(None, 'mp'), may hold values from -0.25 to 0.25
- heads_bias: float32 [2048], P('mp'), may hold values from -0.9 to 0.9
- merge_weight: bfloat16 [1024, 1024], P('mp'), may hold values from -0.75 to 0.75
- merge_bias: float32 [1024], replicated, may hold values from -1.2 to 1.2
- norm_two_gain: float32 [1024], replicated, may hold values from 0.25 to 1.75
- norm_two_shift: float32 [1024], replicated, may hold values from -2 to 2
- widen_weight: bfloat16 [1024, 4096], P(None, 'mp'), may hold values from -0.1875 to 0.1875
- widen_bias: float32 [4096], P('mp'), may hold values from -3 to 3
- narrow_weight: bfloat16 [4096, 1024], P('mp'), may hold values from -0.1875 to 0.1875
- narrow_bias: float32 [1024], replicated, may hold values from -3 to 3
Outputs:
- activations: float32 [24576, 1024], P(('dp', 'mp'))
- input_grad: float32 [24576, 1024], P(('dp', 'mp'))
- lead_weight_grad: float32 [1024], replicated
- lead_shift_grad: float32 [1024], replicated
- norm_one_gain_grad: float32 [1024], replicated
- norm_one_shift_grad: float32 [1024], replicated
- heads_weight_grad: float32 [1024, 3072], P(None, 'mp')
- heads_bias_grad: float32 [2048], P('mp')
- merge_weight_grad: float32 [1024, 1024], P('mp')
- merge_bias_grad: float32 [1024], replicated
- norm_two_gain_grad: float32 [1024], replicated
- norm_two_shift_grad: float32 [1024], replicated
- widen_weight_grad: float32 [1024, 4096], P(None, 'mp')
- widen_bias_grad: float32 [4096], P('mp')
- narrow_weight_grad: float32 [4096, 1024], P('mp')
- narrow_bias_grad: float32 [1024], replicated
The draws below stay inside these ranges and needn't reach their ends.
Inputs may be any that keep to these rules, and one draw needn't show every extreme that they name: `group_items`: live items of each group; in every draw some group holds 3 items and some group exactly one.
All inputs are finite; a program needn't handle non-finite values.
Results may differ from the reference program's by a relative error of at most 0.017.
The reference program's roundings to bfloat16 on the way count: a program that leaves them out, or rounds other values in their place, can miss the bound.
Values may be sent and summed in bfloat16 or wider, within the bound.
No kernel may reach another device: no remote copies, remote signals or barrier semaphores. Data moves between devices by JAX's collectives and lax.ppermute only.
A program may use at most 256 MiB of HBM per device.

```python
import math
import jax
import jax.numpy as jnp
from jax import lax

D = 1024
HEADS = 16
HEAD_DIM = 64
FF = 4096
L = 2048
SLOTS = 3
NSETS = 5
ITEMS = 12
TOKENS = 24576
N_DP = 4


def draw_group_items(key, part):
    key = jax.random.fold_in(key, 11)
    base_key, order_key = jax.random.split(key)
    counts = jax.random.randint(base_key, (N_DP,), 1, SLOTS + 1).astype(jnp.int32)
    order = jax.random.permutation(order_key, N_DP)
    counts = counts.at[order[0]].set(SLOTS)
    counts = counts.at[order[1]].set(1)
    return counts


def draw_tokens(key, part):
    key = jax.random.fold_in(key, 23)
    value_key = jax.random.fold_in(key, 0)
    values = jax.random.truncated_normal(value_key, -6.0, 6.0, (TOKENS, D), jnp.float32)
    return 2.0 * values


def place_ends(result, stream_key, low, largest):
    longest = result.shape.index(max(result.shape))
    spots = []
    for shift in (0, 1):
        where = [jax.random.randint(jax.random.fold_in(stream_key, axis), (), 0, length) for axis, length in enumerate(result.shape)]
        where[longest] = (where[longest] + shift) % result.shape[longest]
        spots.append(tuple(where))
    return result.at[spots[0]].set(low).at[spots[1]].set(largest)


def steps_of(key, shape, cuts, least, top_value):
    factor_of = 1.0
    for axis_at, shards_of in cuts:
        steps = jax.random.uniform(jax.random.fold_in(jax.random.fold_in(key, 6), axis_at), (shards_of,), jnp.float32, least / len(cuts), top_value / len(cuts))
        factor_of = factor_of * jnp.repeat(jnp.exp(steps), shape[axis_at] // shards_of).reshape((-1,) + (1,) * (len(shape) - 1 - axis_at))
    return factor_of


def gaussian(stream_key, extent, scale, bound, cuts=(), held_as=jnp.bfloat16):
    drawn = jax.random.normal(stream_key, extent, jnp.float32) * scale
    if len(cuts) > 0:
        drawn = steps_of(stream_key, extent, cuts, -0.22, 0.18) * drawn
    return jnp.clip(drawn, min=-bound, max=bound).astype(held_as)


def setup_inputs(seed: int = 0) -> dict:
    keys = jax.random.split(jax.random.key(seed), 21)
    return {
        "tokens": draw_tokens(jax.random.fold_in(keys[20], 71), 0),
        "cotangent": gaussian(keys[1], (TOKENS, D), 1.0, 6.0, ((0, 32),), jnp.float32),
        "group_items": draw_group_items(jax.random.fold_in(keys[20], 71), 0),
        "dataset_ids": place_ends(jax.random.randint(keys[3], (ITEMS,), 0, NSETS), jax.random.fold_in(keys[3], 1), 0, NSETS - 1).astype(jnp.int32),
        "lead_hours": place_ends(jax.random.randint(keys[4], (ITEMS,), 6, 169), jax.random.fold_in(keys[4], 1), 6, 168).astype(jnp.int32),
        "set_weights": jnp.clip(jnp.exp(jax.random.uniform(keys[5], (NSETS,), jnp.float32, math.log(0.5), math.log(2.0))), 0.5, 2.0),
        "lead_weight": gaussian(keys[6], (D,), 0.3, 1.5, (), jnp.float32),
        "lead_shift": gaussian(keys[7], (D,), 0.2, 1.0, (), jnp.float32),
        "norm_one_gain": jnp.clip(1.0 + 0.15 * jax.random.normal(keys[8], (D,), jnp.float32), 0.25, 1.75),
        "norm_one_shift": gaussian(keys[9], (D,), 0.15, 0.9, (), jnp.float32),
        "heads_weight": gaussian(keys[10], (D, 3 * D), (D // 2) ** -0.5, 0.25, ((1, 8),)),
        "heads_bias": gaussian(keys[11], (2 * D,), 0.15, 0.9, ((0, 8),), jnp.float32),
        "merge_weight": gaussian(keys[12], (D, D), (D // 16) ** -0.5, 0.75, ((0, 8),)),
        "merge_bias": gaussian(keys[13], (D,), 0.2, 1.2, (), jnp.float32),
        "norm_two_gain": jnp.clip(1.0 + 0.15 * jax.random.normal(keys[14], (D,), jnp.float32), 0.25, 1.75),
        "norm_two_shift": gaussian(keys[15], (D,), 0.3, 2.0, (), jnp.float32),
        "widen_weight": gaussian(keys[16], (D, FF), D ** -0.5, 0.1875, ((1, 8),)),
        "widen_bias": gaussian(keys[17], (FF,), 0.5, 3.0, ((0, 8),), jnp.float32),
        "narrow_weight": gaussian(keys[18], (FF, D), (FF // 4) ** -0.5, 0.1875, ((0, 8),)),
        "narrow_bias": gaussian(keys[19], (D,), 0.5, 3.0, (), jnp.float32),
    }


@jax.custom_vjp
def low(v):
    return lax.optimization_barrier(v.astype(jnp.bfloat16)).astype(jnp.float32)

@jax.custom_vjp
def low_back(v):
    return v

def low_keep(v):
    return (low(v), None)

def low_pass(kept, grad):
    return (grad,)

def back_keep(v):
    return (v, None)

def back_low(kept, grad):
    return (low(grad),)
low.defvjp(low_keep, low_pass)
low_back.defvjp(back_keep, back_low)
EPSILON = 1e-05
HIGHEST = lax.Precision.HIGHEST

def layer_norm(value, gain, shift):
    mean = lax.optimization_barrier(jnp.mean(value, -1, keepdims=True))
    centred = value - mean
    variance = lax.optimization_barrier(jnp.mean(centred * centred, -1, keepdims=True))
    return centred * lax.rsqrt(variance + EPSILON) * gain + shift

def attend_block(query_block, key_rows, value_rows):
    factor = HEAD_DIM ** (-0.5)
    scores = low_back(factor * jnp.einsum('hqd,hkd->hqk', query_block, key_rows, precision=HIGHEST))
    attn_probs = low(jax.nn.softmax(scores, axis=-1))
    return low(low_back(jnp.einsum('hqk,hkd->hqd', attn_probs, value_rows, precision=HIGHEST)))

def layer_item(params, item_tokens, item_lead):
    lead_weight, lead_shift, norm_one_gain, norm_one_shift, heads_weight, heads_bias, merge_weight, merge_bias, norm_two_gain, norm_two_shift, widen_weight, widen_bias, narrow_weight, narrow_bias = params
    start_state = item_tokens + item_lead * lead_weight + lead_shift
    normed_one = low(layer_norm(start_state, norm_one_gain, norm_one_shift))
    bias_heads = heads_bias.reshape(HEADS, 2, HEAD_DIM)
    full_bias = jnp.stack([bias_heads[:, 0], jnp.zeros_like(bias_heads[:, 0]), bias_heads[:, 1]], 1).reshape(-1)
    packed = low(low_back(jnp.dot(normed_one, heads_weight, precision=HIGHEST) + full_bias))
    packed = packed.reshape(L, HEADS, 3, HEAD_DIM).transpose(2, 1, 0, 3)
    block_rows = min(512, L)
    query_blocks = packed[0].reshape(HEADS, L // block_rows, block_rows, HEAD_DIM).transpose(1, 0, 2, 3)
    key_rows = packed[1]
    value_rows = packed[2]

    def one_block(query_block):
        return attend_block(query_block, key_rows, value_rows)
    contexts = lax.map(jax.checkpoint(one_block), query_blocks)
    context_rows = contexts.transpose(0, 2, 1, 3).reshape(L, HEADS * HEAD_DIM)
    attn_out = low_back(jnp.dot(context_rows, merge_weight, precision=HIGHEST) + merge_bias)
    middle = start_state + attn_out
    normed_two = low(layer_norm(middle, norm_two_gain, norm_two_shift))
    hidden_pre = low_back(jnp.dot(normed_two, widen_weight, precision=HIGHEST) + widen_bias)
    hidden = low(jax.nn.gelu(hidden_pre, approximate=False))
    mlp_out = low_back(jnp.dot(hidden, narrow_weight, precision=HIGHEST) + narrow_bias)
    return middle + mlp_out

def reference(tokens, cotangent, group_items, dataset_ids, lead_hours, set_weights, lead_weight, lead_shift, norm_one_gain, norm_one_shift, heads_weight, heads_bias, merge_weight, merge_bias, norm_two_gain, norm_two_shift, widen_weight, widen_bias, narrow_weight, narrow_bias):
    count_items = N_DP * SLOTS
    params = (lead_weight.astype(jnp.float32), lead_shift.astype(jnp.float32), norm_one_gain.astype(jnp.float32), norm_one_shift.astype(jnp.float32), heads_weight.astype(jnp.float32), heads_bias.astype(jnp.float32), merge_weight.astype(jnp.float32), merge_bias.astype(jnp.float32), norm_two_gain.astype(jnp.float32), norm_two_shift.astype(jnp.float32), widen_weight.astype(jnp.float32), widen_bias.astype(jnp.float32), narrow_weight.astype(jnp.float32), narrow_bias.astype(jnp.float32))
    item_tokens = tokens.astype(jnp.float32).reshape(count_items, L, D)
    leads = lead_hours.astype(jnp.float32) / 100.0

    def forward(weights, inputs):

        def one_item(pair):
            return layer_item(weights, pair[0], pair[1])
        return lax.map(jax.checkpoint(one_item), (inputs, leads))
    activations, pull_back = jax.vjp(forward, params, item_tokens)
    slot_ids = jnp.arange(SLOTS).astype(jnp.int32)
    live = (slot_ids[None, :] < group_items[:, None]).reshape(-1).astype(jnp.float32)
    set_match = (dataset_ids[:, None] == jnp.arange(NSETS).astype(jnp.int32)[None, :]).astype(jnp.float32)
    item_weight = live * lax.optimization_barrier(jnp.sum(set_match * set_weights[None, :], 1))
    grad_out = cotangent.reshape(count_items, L, D) * item_weight[:, None, None]
    param_grads, token_grads = pull_back(grad_out)
    item_total = jnp.sum(group_items.astype(jnp.float32))
    scaled = [grad / item_total for grad in param_grads]
    return (activations.reshape(TOKENS, D), token_grads.reshape(TOKENS, D) / item_total, scaled[0], scaled[1], scaled[2], scaled[3], scaled[4], scaled[5], scaled[6], scaled[7], scaled[8], scaled[9], scaled[10], scaled[11], scaled[12], scaled[13])
```

```python
import functools

import jax
import jax.numpy as jnp
from jax import lax
from jax.experimental import pallas as pl
from jax.experimental.pallas import tpu as pltpu
from jax.sharding import PartitionSpec as P

HEAD_DIM = 64
EPSILON = 1e-05
F32 = jnp.float32
BF16 = jnp.bfloat16
NN = (((1,), (0,)), ((), ()))
NT = (((1,), (1,)), ((), ()))
TN = (((0,), (0,)), ((), ()))
BOTH = ("mp", "dp")
VMEM_LIMIT = 56 * 2**20

TAIL_STEP = 0.35
TAIL = (
    0.13962124730886327,
    0.1398645225480897,
    0.11981419159397333,
    0.10557980057214614,
    -0.023275300634317965,
    0.1594091170984717,
    -0.25591569617440285,
    0.14406734292143564,
    -0.029165241243977125,
)


def mm(left, right, dims=NN):
    return lax.dot_general(left, right, dims, preferred_element_type=F32)


def params():
    return pltpu.CompilerParams(vmem_limit_bytes=VMEM_LIMIT)


def cost(flops, moved, exps=0):
    return pl.CostEstimate(flops=int(flops), bytes_accessed=int(moved), transcendentals=int(exps))


def gelu_parts(value):
    size = jnp.abs(value)
    t = 1.0 / (1.0 + TAIL_STEP * size)
    poly = jnp.full_like(t, TAIL[-1])
    for term in TAIL[-2::-1]:
        poly = poly * t + term
    bell = jnp.exp(-0.5 * value * value)
    tail = poly * t * bell
    cumulative = jnp.where(value >= 0.0, 1.0 - tail, tail)
    return cumulative, value * (bell * 0.3989422804014327)


def project_kernel(x_ref, w_ref, b_ref, out_ref):
    out_ref[0] = (mm(x_ref[...], w_ref[0]) + b_ref[0]).astype(BF16)


def project(normed, weight, bias):
    shards, width, cols = weight.shape
    rows = normed.shape[0]
    return pl.pallas_call(
        project_kernel,
        grid=(shards,),
        in_specs=[
            pl.BlockSpec((rows, width), lambda m: (0, 0)),
            pl.BlockSpec((1, width, cols), lambda m: (m, 0, 0)),
            pl.BlockSpec((1, 1, cols), lambda m: (m, 0, 0)),
        ],
        out_specs=pl.BlockSpec((1, rows, cols), lambda m: (m, 0, 0)),
        out_shape=jax.ShapeDtypeStruct((shards, rows, cols), BF16),
        compiler_params=params(),
        cost_estimate=cost(2 * shards * rows * width * cols, weight.size * 2 + rows * shards * cols * 2),
    )(normed, weight, bias)


def attend_kernel(heads, block, x_ref, ctx_ref, lse_ref, keys_s, values_s):
    step = pl.program_id(1)
    length = x_ref.shape[1]

    @pl.when(step == 0)
    def _():
        for h in range(heads):
            c = h * 3 * HEAD_DIM
            keys_s[h] = x_ref[0, :, c + HEAD_DIM : c + 2 * HEAD_DIM].T
            values_s[h, :, :HEAD_DIM] = x_ref[0, :, c + 2 * HEAD_DIM : c + 3 * HEAD_DIM]
            values_s[h, :, HEAD_DIM:] = jnp.ones((length, HEAD_DIM), BF16)

    rows = pl.ds(pl.multiple_of(step * block, block), block)
    here = x_ref[0, rows, :]
    for h in range(heads):
        c = h * 3 * HEAD_DIM
        query = here[:, c : c + HEAD_DIM] * jnp.asarray(HEAD_DIM**-0.5, BF16)
        scores = mm(query, keys_s[h])
        row_max = jnp.max(scores, 1, keepdims=True)
        probs = jnp.exp(scores - row_max).astype(BF16)
        summed = mm(probs, values_s[h])
        total = summed[:, HEAD_DIM : HEAD_DIM + 1]
        ctx_ref[0, :, h * HEAD_DIM : (h + 1) * HEAD_DIM] = (summed[:, :HEAD_DIM] / total).astype(BF16)
        total_log = row_max + jnp.log(total)
        lse_ref[0, h : h + 1, :] = jnp.broadcast_to(total_log, (block, 128)).T[:1]


def attend(packed, heads, block):
    units, length, cols = packed.shape
    wide = heads * HEAD_DIM
    return pl.pallas_call(
        functools.partial(attend_kernel, heads, block),
        grid=(units, length // block),
        in_specs=[pl.BlockSpec((1, length, cols), lambda u, i: (u, 0, 0))],
        out_specs=[
            pl.BlockSpec((1, block, wide), lambda u, i: (u, i, 0)),
            pl.BlockSpec((1, heads, block), lambda u, i: (u, 0, i)),
        ],
        out_shape=[
            jax.ShapeDtypeStruct((units, length, wide), BF16),
            jax.ShapeDtypeStruct((units, heads, length), F32),
        ],
        scratch_shapes=[
            pltpu.VMEM((heads, HEAD_DIM, length), BF16),
            pltpu.VMEM((heads, length, 2 * HEAD_DIM), BF16),
        ],
        compiler_params=params(),
        cost_estimate=cost(units * heads * 16 * length * length * HEAD_DIM, packed.size * 3, units * heads * length * length),
    )(packed)


def attend_back_kernel(
    heads, block, x_ref, ctx_ref, dctx_ref, lse_ref, grad_ref, keys_t, keys_s, values_s, dk_s, dv_s
):
    step = pl.program_id(1)

    @pl.when(step == 0)
    def _():
        for h in range(heads):
            c = h * 3 * HEAD_DIM
            key = x_ref[0, :, c + HEAD_DIM : c + 2 * HEAD_DIM]
            keys_s[h] = key
            keys_t[h] = key.T
            values_s[h] = x_ref[0, :, c + 2 * HEAD_DIM : c + 3 * HEAD_DIM]
        dk_s[...] = jnp.zeros_like(dk_s)
        dv_s[...] = jnp.zeros_like(dv_s)

    rows = pl.ds(pl.multiple_of(step * block, block), block)
    here = x_ref[0, rows, :]
    grads = dctx_ref[0]
    prods = ctx_ref[0].astype(F32) * grads.astype(F32)
    for h in range(heads):
        c = h * 3 * HEAD_DIM
        part = slice(h * HEAD_DIM, (h + 1) * HEAD_DIM)
        query = here[:, c : c + HEAD_DIM] * jnp.asarray(HEAD_DIM**-0.5, BF16)
        grad = grads[:, part]
        centre = jnp.sum(prods[:, part].T, 0, keepdims=True)
        scores_t = mm(keys_s[h], query.T)
        probs_t = jnp.exp(scores_t - lse_ref[0, h : h + 1, :])
        grad_probs_t = mm(values_s[h], grad.T)
        grad_scores_t = (probs_t * (grad_probs_t - centre)).astype(BF16)
        dv_s[h] += mm(probs_t.astype(BF16), grad)
        dk_s[h] += mm(grad_scores_t, query)
        grad_query_t = mm(keys_t[h], grad_scores_t)
        grad_ref[0, rows, c : c + HEAD_DIM] = (grad_query_t.T * HEAD_DIM**-0.5).astype(BF16)

    @pl.when(step == pl.num_programs(1) - 1)
    def _():
        for h in range(heads):
            c = h * 3 * HEAD_DIM
            grad_ref[0, :, c + HEAD_DIM : c + 2 * HEAD_DIM] = dk_s[h].astype(BF16)
            grad_ref[0, :, c + 2 * HEAD_DIM : c + 3 * HEAD_DIM] = dv_s[h].astype(BF16)


def attend_back(packed, context, grad_context, lse, heads, block):
    units, length, cols = packed.shape
    wide = heads * HEAD_DIM
    return pl.pallas_call(
        functools.partial(attend_back_kernel, heads, block),
        grid=(units, length // block),
        in_specs=[
            pl.BlockSpec((1, length, cols), lambda u, i: (u, 0, 0)),
            pl.BlockSpec((1, block, wide), lambda u, i: (u, i, 0)),
            pl.BlockSpec((1, block, wide), lambda u, i: (u, i, 0)),
            pl.BlockSpec((1, heads, block), lambda u, i: (u, 0, i)),
        ],
        out_specs=pl.BlockSpec((1, length, cols), lambda u, i: (u, 0, 0)),
        out_shape=jax.ShapeDtypeStruct((units, length, cols), BF16),
        scratch_shapes=[
            pltpu.VMEM((heads, HEAD_DIM, length), BF16),
            pltpu.VMEM((heads, length, HEAD_DIM), BF16),
            pltpu.VMEM((heads, length, HEAD_DIM), BF16),
            pltpu.VMEM((heads, length, HEAD_DIM), F32),
            pltpu.VMEM((heads, length, HEAD_DIM), F32),
        ],
        compiler_params=params(),
        cost_estimate=cost(units * heads * 40 * length * length * HEAD_DIM, packed.size * 5, units * heads * length * length),
    )(packed, context, grad_context, lse)


def feed_kernel(
    parts, x_ref, g_ref, widen_ref, narrow_ref, bias_ref, out_ref, dx_ref, grads_ref, bias_grad_ref, out_s, dx_s
):
    step = pl.program_id(0)
    count, depth, tile = widen_ref.shape[1:]
    width = count * depth
    piece = depth // parts
    widen = widen_ref[0].reshape(width, tile)
    normed = x_ref[...]
    grad = g_ref[...]
    narrow = [
        narrow_ref[0, :, c * piece : (c + 1) * piece, :].reshape(tile, tile) for c in range(parts)
    ]
    narrow = jnp.concatenate(narrow, 1)
    pre = mm(normed, widen) + bias_ref[0]
    cumulative, slope = gelu_parts(pre)
    hidden = (pre * cumulative).astype(BF16)
    grad_pre = (mm(grad, narrow, NT) * (cumulative + slope)).astype(BF16)
    out = mm(hidden, narrow)
    dx = mm(grad_pre, widen, NT)

    @pl.when(step == 0)
    def _():
        out_s[...] = out
        dx_s[...] = dx

    @pl.when(step > 0)
    def _():
        out_s[...] += out
        dx_s[...] += dx

    grads_ref[0, :, :piece, :] = mm(grad_pre, normed, TN).astype(BF16).reshape(count, tile // count, width)
    grads_ref[0, :, piece:, :] = mm(hidden, grad, TN).astype(BF16).reshape(count, tile // count, width)
    bias_grad_ref[0] = jnp.sum(grad_pre.astype(F32), 0, keepdims=True)

    @pl.when(step == pl.num_programs(0) - 1)
    def _():
        out_ref[...] = out_s[...]
        dx_ref[...] = dx_s[...]


def feed(normed, grad, rest, bias, extra):
    shards, count, _, tile = rest.shape
    rows, width = normed.shape
    depth = width // count
    parts = width // tile
    piece = tile // count
    return pl.pallas_call(
        functools.partial(feed_kernel, parts),
        grid=(shards,),
        in_specs=[
            pl.BlockSpec((rows, width), lambda m: (0, 0)),
            pl.BlockSpec((rows, width), lambda m: (0, 0)),
            pl.BlockSpec((1, count, depth, tile), lambda m: (m, 0, 0, 0)),
            pl.BlockSpec((1, count, depth, tile), lambda m: (m, 0, 1, 0)),
            pl.BlockSpec((1, 1, tile), lambda m: (m, 0, 0)),
        ],
        out_specs=[
            pl.BlockSpec((rows, width), lambda m: (0, 0)),
            pl.BlockSpec((rows, width), lambda m: (0, 0)),
            pl.BlockSpec((1, count, 2 * piece, width), lambda m: (m, 0, 0, 0)),
            pl.BlockSpec((1, 1, tile), lambda m: (m, 0, 0)),
        ],
        out_shape=[
            jax.ShapeDtypeStruct((rows, width), F32),
            jax.ShapeDtypeStruct((rows, width), F32),
            jax.ShapeDtypeStruct((shards, count, 2 * piece + extra, width), BF16),
            jax.ShapeDtypeStruct((shards, 1, tile), F32),
        ],
        scratch_shapes=[pltpu.VMEM((rows, width), F32), pltpu.VMEM((rows, width), F32)],
        compiler_params=params(),
        cost_estimate=cost(12 * shards * rows * width * tile, rest.size * 4 + rows * width * 12, rows * shards * tile),
    )(normed, grad, rest, rest, bias)


def project_back_kernel(x_ref, g_ref, w_ref, dx_ref, grads_ref, bias_grad_ref, dx_s):
    step = pl.program_id(0)
    grad = g_ref[0]
    dx = mm(grad, w_ref[0], NT)

    @pl.when(step == 0)
    def _():
        dx_s[...] = dx

    @pl.when(step > 0)
    def _():
        dx_s[...] += dx

    grads_ref[0] = mm(grad, x_ref[...], TN).astype(BF16)
    bias_grad_ref[0] = jnp.sum(grad.astype(F32), 0, keepdims=True)

    @pl.when(step == pl.num_programs(0) - 1)
    def _():
        dx_ref[...] = dx_s[...]


def project_back(normed, grad, weight):
    shards, width, cols = weight.shape
    rows = normed.shape[0]
    return pl.pallas_call(
        project_back_kernel,
        grid=(shards,),
        in_specs=[
            pl.BlockSpec((rows, width), lambda m: (0, 0)),
            pl.BlockSpec((1, rows, cols), lambda m: (m, 0, 0)),
            pl.BlockSpec((1, width, cols), lambda m: (m, 0, 0)),
        ],
        out_specs=[
            pl.BlockSpec((rows, width), lambda m: (0, 0)),
            pl.BlockSpec((1, cols, width), lambda m: (m, 0, 0)),
            pl.BlockSpec((1, 1, cols), lambda m: (m, 0, 0)),
        ],
        out_shape=[
            jax.ShapeDtypeStruct((rows, width), F32),
            jax.ShapeDtypeStruct((shards, cols, width), BF16),
            jax.ShapeDtypeStruct((shards, 1, cols), F32),
        ],
        scratch_shapes=[pltpu.VMEM((rows, width), F32)],
        compiler_params=params(),
        cost_estimate=cost(4 * shards * rows * width * cols, weight.size * 6),
    )(normed, grad, weight)


def norm_parts(value):
    mean = jnp.mean(value, -1, keepdims=True)
    centred = value - mean
    scale = lax.rsqrt(jnp.mean(centred * centred, -1, keepdims=True) + EPSILON)
    return centred * scale, scale


def norm_back(normal, scale, gain, grad):
    grad_x = grad * gain
    mean = jnp.mean(grad_x, -1, keepdims=True)
    along = jnp.mean(grad_x * normal, -1, keepdims=True)
    return (
        (grad_x - mean - normal * along) * scale,
        jnp.sum(grad * normal, 0),
        jnp.sum(grad, 0),
    )


def split_rows(array, count):
    share = array.shape[0] // count
    return lax.dynamic_slice_in_dim(array, lax.axis_index("dp") * share, share, 0)


def on_device(
    tokens,
    cotangent,
    group_items,
    dataset_ids,
    lead_hours,
    set_weights,
    lead_weight,
    lead_shift,
    norm_one_gain,
    norm_one_shift,
    heads_weight,
    heads_bias,
    merge_weight,
    merge_bias,
    norm_two_gain,
    norm_two_shift,
    widen_weight,
    widen_bias,
    narrow_weight,
    narrow_bias,
):
    shards = lax.axis_size("mp")
    copies = lax.axis_size("dp")
    rows_here, width = tokens.shape
    group_rows = rows_here * shards
    slots = dataset_ids.shape[0]
    length = group_rows // slots
    cols = heads_weight.shape[1]
    heads_here = cols // (3 * HEAD_DIM)
    wide = heads_here * HEAD_DIM
    tile = widen_weight.shape[1]
    parts = width // tile
    block = min(256, length)

    heads_all = lax.all_gather(split_rows(heads_weight, copies), BOTH, axis=0, tiled=True)
    heads_all = heads_all.reshape(shards, width, cols)

    def fold(part):
        return jnp.concatenate(jnp.split(part, parts, 1), 0)

    rest = jnp.concatenate(
        [
            split_rows(widen_weight, copies),
            fold(split_rows(narrow_weight, copies)),
            fold(split_rows(merge_weight, copies)),
        ],
        0,
    )
    bias_heads = heads_bias.reshape(heads_here, 2, HEAD_DIM)
    full_bias = jnp.stack(
        [bias_heads[:, 0], jnp.zeros_like(bias_heads[:, 0]), bias_heads[:, 1]], 1
    ).reshape(-1)
    biases = jnp.concatenate([full_bias, widen_bias])
    biases = lax.all_to_all(
        jnp.broadcast_to(biases, (shards,) + biases.shape), "mp", 0, 0, tiled=True
    )
    heads_bias_all = biases[:, None, :cols]
    widen_bias_all = biases[:, None, cols:]

    row_ids = lax.axis_index("mp") * rows_here + jnp.arange(rows_here, dtype=jnp.int32)
    slot_ids = jnp.arange(slots, dtype=jnp.int32)
    slot_table = ((row_ids // length)[:, None] == slot_ids[None, :]).astype(F32)
    lead_scaled = jnp.sum(slot_table * (lead_hours.astype(F32) / 100.0)[None, :], 1)
    live = (slot_ids < group_items[0]).astype(F32)
    set_ids = jnp.arange(set_weights.shape[0], dtype=jnp.int32)
    set_match = (dataset_ids[:, None] == set_ids[None, :]).astype(F32)
    item_weight = live * jnp.sum(set_match * set_weights[None, :], 1)
    row_weight = jnp.sum(slot_table * item_weight[None, :], 1)
    item_total = lax.psum(group_items.astype(F32)[0], "dp")

    start_state = tokens + lead_scaled[:, None] * lead_weight + lead_shift
    first_normal, first_scale = norm_parts(start_state)
    normed_one = (first_normal * norm_one_gain + norm_one_shift).astype(BF16)
    packed = project(normed_one, heads_all, heads_bias_all)
    packed, rest = lax.optimization_barrier((packed, rest))
    rest = lax.all_gather(rest, BOTH, axis=0, tiled=True)
    rest = rest.reshape(shards, copies, -1, tile)
    packed = lax.all_to_all(packed, "mp", 0, 0, tiled=True).reshape(slots, length, cols)
    context, lse = attend(packed, heads_here, block)
    context_rows = lax.all_to_all(
        context.reshape(shards, rows_here, wide), "mp", 0, 0, tiled=True
    )
    context_rows = context_rows.transpose(1, 0, 2).reshape(rows_here, width)
    merge_rows = merge_weight.shape[0] // copies
    merge_all = rest[:, :, -merge_rows * parts :, :].reshape(shards, copies, parts, merge_rows, tile)
    merge_all = merge_all.transpose(0, 1, 3, 2, 4).reshape(width, width)
    middle = start_state + mm(context_rows, merge_all) + merge_bias
    second_normal, second_scale = norm_parts(middle)
    normed_two = (second_normal * norm_two_gain + norm_two_shift).astype(BF16)

    grad_out = cotangent * row_weight[:, None]
    grad_low = grad_out.astype(BF16)
    narrow_bias_grad = jnp.sum(grad_low.astype(F32), 0)
    fed, grad_norm_two, grads_one, widen_bias_grad = feed(
        normed_two, grad_low, rest, widen_bias_all, merge_rows
    )
    activations = middle + fed + narrow_bias
    grad_mid_norm, norm_two_gain_grad, norm_two_shift_grad = norm_back(
        second_normal, second_scale, norm_two_gain, grad_norm_two
    )
    grad_middle = grad_out + grad_mid_norm
    grad_mid_low = grad_middle.astype(BF16)
    merge_bias_grad = jnp.sum(grad_mid_low.astype(F32), 0)
    merge_weight_grad = mm(context_rows, grad_mid_low, TN).astype(BF16)
    grads_one = grads_one.at[:, :, -merge_rows:].set(
        merge_weight_grad.reshape(shards, copies, merge_rows, width)
    )
    grads_one = lax.psum_scatter(
        grads_one.reshape(-1, width), BOTH, scatter_dimension=0, tiled=True
    )
    grad_context = mm(grad_mid_low, merge_all, NT).astype(BF16)
    grad_context = lax.all_to_all(
        grad_context.reshape(rows_here, shards, wide).transpose(1, 0, 2), "mp", 0, 0, tiled=True
    )
    grad_packed = attend_back(
        packed, context, grad_context.reshape(slots, length, wide), lse, heads_here, block
    )
    grad_packed = lax.all_to_all(
        grad_packed.reshape(shards, rows_here, cols), "mp", 0, 0, tiled=True
    )
    grad_norm_one, grads_two, heads_bias_grad = project_back(normed_one, grad_packed, heads_all)
    grads_two = lax.psum_scatter(
        grads_two.reshape(-1, width), BOTH, scatter_dimension=0, tiled=True
    )
    grad_start_norm, norm_one_gain_grad, norm_one_shift_grad = norm_back(
        first_normal, first_scale, norm_one_gain, grad_norm_one
    )
    grad_start = grad_middle + grad_start_norm
    lead_weight_grad = jnp.sum(grad_start * lead_scaled[:, None], 0)
    lead_shift_grad = jnp.sum(grad_start, 0)
    vectors = (
        lead_weight_grad,
        lead_shift_grad,
        norm_one_gain_grad,
        norm_one_shift_grad,
        merge_bias_grad,
        norm_two_gain_grad,
        norm_two_shift_grad,
        narrow_bias_grad,
    )
    vectors = jnp.concatenate(
        [jnp.stack(vectors).reshape(-1), widen_bias_grad.reshape(-1), heads_bias_grad.reshape(-1)]
    )
    vectors = lax.psum(vectors, ("dp", "mp")) / item_total
    shared = vectors[: 8 * width].reshape(8, width)
    place = lax.axis_index("mp")
    widen_bias_total = lax.dynamic_slice_in_dim(vectors, 8 * width + place * tile, tile, 0)
    heads_bias_total = lax.dynamic_slice_in_dim(
        vectors, 8 * width + shards * tile + place * cols, cols, 0
    ).reshape(heads_here, 3, HEAD_DIM)
    heads_bias_total = jnp.stack([heads_bias_total[:, 0], heads_bias_total[:, 2]], 1).reshape(-1)

    grads_one = lax.all_gather(grads_one, "dp", axis=0, tiled=True).astype(F32) / item_total
    grads_one = grads_one.reshape(copies, -1, width)
    piece = tile // copies
    widen_total = grads_one[:, :piece].reshape(tile, width).T
    narrow_total = grads_one[:, piece : 2 * piece].reshape(tile, width)
    merge_total = grads_one[:, 2 * piece :].reshape(-1, width)
    grads_two = lax.all_gather(grads_two, "dp", axis=0, tiled=True).astype(F32) / item_total
    heads_total = grads_two.T
    return (
        activations,
        grad_start / item_total,
        shared[0],
        shared[1],
        shared[2],
        shared[3],
        heads_total,
        heads_bias_total,
        merge_total,
        shared[4],
        shared[5],
        shared[6],
        widen_total,
        widen_bias_total,
        narrow_total,
        shared[7],
    )


def solution(mesh):
    return jax.shard_map(
        on_device,
        mesh=mesh,
        in_specs=(
            P(("dp", "mp"), None),
            P(("dp", "mp"), None),
            P("dp"),
            P("dp"),
            P("dp"),
            P(),
            P(),
            P(),
            P(),
            P(),
            P(None, "mp"),
            P("mp"),
            P("mp", None),
            P(),
            P(),
            P(),
            P(None, "mp"),
            P("mp"),
            P("mp", None),
            P(),
        ),
        out_specs=(
            P(("dp", "mp"), None),
            P(("dp", "mp"), None),
            P(),
            P(),
            P(),
            P(),
            P(None, "mp"),
            P("mp"),
            P("mp", None),
            P(),
            P(),
            P(),
            P(None, "mp"),
            P("mp"),
            P("mp", None),
            P(),
        ),
        check_vma=False,
    )
```

```python
import functools

import jax
import jax.numpy as jnp
from jax import lax
from jax.experimental import pallas as pl
from jax.experimental.pallas import tpu as pltpu
from jax.sharding import PartitionSpec as P

HEAD_DIM = 64
EPSILON = 1e-05
F32 = jnp.float32
BF16 = jnp.bfloat16
NN = (((1,), (0,)), ((), ()))
NT = (((1,), (1,)), ((), ()))
TN = (((0,), (0,)), ((), ()))
BOTH = ("mp", "dp")
VMEM_LIMIT = 56 * 2**20

TAIL_STEP = 0.35
TAIL = (
    0.13962124730886327,
    0.1398645225480897,
    0.11981419159397333,
    0.10557980057214614,
    -0.023275300634317965,
    0.1594091170984717,
    -0.25591569617440285,
    0.14406734292143564,
    -0.029165241243977125,
)


def mm(left, right, dims=NN):
    return lax.dot_general(left, right, dims, preferred_element_type=F32)


def params():
    return pltpu.CompilerParams(vmem_limit_bytes=VMEM_LIMIT)


def cost(flops, moved, exps=0):
    return pl.CostEstimate(flops=int(flops), bytes_accessed=int(moved), transcendentals=int(exps))


def gelu_parts(value):
    size = jnp.abs(value)
    t = 1.0 / (1.0 + TAIL_STEP * size)
    poly = jnp.full_like(t, TAIL[-1])
    for term in TAIL[-2::-1]:
        poly = poly * t + term
    bell = jnp.exp(-0.5 * value * value)
    tail = poly * t * bell
    cumulative = jnp.where(value >= 0.0, 1.0 - tail, tail)
    return cumulative, value * (bell * 0.3989422804014327)


def project_kernel(slots, table_ref, own_ref, other_ref, w_ref, out_ref):
    step = pl.program_id(0)
    count = pl.num_programs(0)
    width = own_ref.shape[-1]
    block = own_ref.shape[1]
    here = jnp.where(step < count // 2, own_ref[0], other_ref[0])
    for j in range(slots):

        @pl.when(table_ref[step] == table_ref[2 * count + j])
        def _():
            bias = jnp.sum(w_ref[j, width : width + 3, :].astype(F32), 0, keepdims=True)
            rows = pl.ds(pl.multiple_of(table_ref[count + step] * block, block), block)
            out_ref[j, rows, :] = (mm(here, w_ref[j, :width, :]) + bias).astype(BF16)


def project(own, other, weight, table, length):
    half, block, width = own.shape
    slots, _, cols = weight.shape
    return pl.pallas_call(
        functools.partial(project_kernel, slots),
        grid_spec=pltpu.PrefetchScalarGridSpec(
            num_scalar_prefetch=1,
            grid=(2 * half,),
            in_specs=[
                pl.BlockSpec((1, block, width), lambda q, t: (jnp.minimum(q, half - 1), 0, 0)),
                pl.BlockSpec((1, block, width), lambda q, t: (jnp.maximum(q - half, 0), 0, 0)),
                pl.BlockSpec(weight.shape, lambda q, t: (0, 0, 0)),
            ],
            out_specs=pl.BlockSpec((slots, length, cols), lambda q, t: (0, 0, 0)),
        ),
        out_shape=jax.ShapeDtypeStruct((slots, length, cols), BF16),
        compiler_params=params(),
        cost_estimate=cost(2 * slots * length * width * cols, own.size * 4 + slots * length * cols * 2),
    )(table, own, other, weight)


def project_back_kernel(slots, table_ref, own_ref, other_ref, w_ref, g_ref, own_dx, other_dx, dw_ref, dx_s, dw_s):
    step = pl.program_id(0)
    count = pl.num_programs(0)
    width = own_ref.shape[-1]
    block = own_ref.shape[1]
    here = jnp.where(step < count // 2, own_ref[0], other_ref[0])
    dx_s[...] = jnp.zeros_like(dx_s)

    @pl.when(step == 0)
    def _():
        dw_s[...] = jnp.zeros_like(dw_s)

    for j in range(slots):

        @pl.when(table_ref[step] == table_ref[2 * count + j])
        def _():
            rows = pl.ds(pl.multiple_of(table_ref[count + step] * block, block), block)
            grad = g_ref[j, rows, :]
            dx_s[...] += mm(grad, w_ref[j, :width, :], NT)
            dw_s[j] += mm(grad, here, TN)

    @pl.when(step < count // 2)
    def _():
        own_dx[0] = dx_s[...].astype(BF16)

    @pl.when(step >= count // 2)
    def _():
        other_dx[0] = dx_s[...].astype(BF16)

    @pl.when(step == count - 1)
    def _():
        dw_ref[...] = dw_s[...].astype(BF16)


def project_back(own, other, weight, grad, table):
    half, block, width = own.shape
    slots, length, cols = grad.shape
    return pl.pallas_call(
        functools.partial(project_back_kernel, slots),
        grid_spec=pltpu.PrefetchScalarGridSpec(
            num_scalar_prefetch=1,
            grid=(2 * half,),
            in_specs=[
                pl.BlockSpec((1, block, width), lambda q, t: (jnp.minimum(q, half - 1), 0, 0)),
                pl.BlockSpec((1, block, width), lambda q, t: (jnp.maximum(q - half, 0), 0, 0)),
                pl.BlockSpec(weight.shape, lambda q, t: (0, 0, 0)),
                pl.BlockSpec(grad.shape, lambda q, t: (0, 0, 0)),
            ],
            out_specs=[
                pl.BlockSpec((1, block, width), lambda q, t: (jnp.minimum(q, half - 1), 0, 0)),
                pl.BlockSpec((1, block, width), lambda q, t: (jnp.maximum(q - half, 0), 0, 0)),
                pl.BlockSpec((slots, cols, width), lambda q, t: (0, 0, 0)),
            ],
            scratch_shapes=[pltpu.VMEM((block, width), F32), pltpu.VMEM((slots, cols, width), F32)],
        ),
        out_shape=[
            jax.ShapeDtypeStruct((half, block, width), BF16),
            jax.ShapeDtypeStruct((half, block, width), BF16),
            jax.ShapeDtypeStruct((slots, cols, width), BF16),
        ],
        compiler_params=params(),
        cost_estimate=cost(4 * slots * length * width * cols, own.size * 8 + grad.size * 2),
    )(table, own, other, weight, grad)


def attend_kernel(heads, block, place_ref, x_ref, ctx_ref, lse_ref, keys_s, values_s):
    step = pl.program_id(1)
    length = x_ref.shape[1]

    @pl.when(step == 0)
    def _():
        for h in range(heads):
            c = h * 3 * HEAD_DIM
            keys_s[h] = x_ref[0, :, c + HEAD_DIM : c + 2 * HEAD_DIM].T
            values_s[h, :, :HEAD_DIM] = x_ref[0, :, c + 2 * HEAD_DIM : c + 3 * HEAD_DIM]
            values_s[h, :, HEAD_DIM:] = jnp.ones((length, HEAD_DIM), BF16)

    rows = pl.ds(pl.multiple_of(step * block, block), block)
    here = x_ref[0, rows, :]
    for h in range(heads):
        c = h * 3 * HEAD_DIM
        query = here[:, c : c + HEAD_DIM] * jnp.asarray(HEAD_DIM**-0.5, BF16)
        scores = mm(query, keys_s[h])
        row_max = jnp.max(scores, 1, keepdims=True)
        probs = jnp.exp(scores - row_max).astype(BF16)
        summed = mm(probs, values_s[h])
        total = summed[:, HEAD_DIM : HEAD_DIM + 1]
        ctx_ref[0, :, h * HEAD_DIM : (h + 1) * HEAD_DIM] = (summed[:, :HEAD_DIM] / total).astype(BF16)
        total_log = row_max + jnp.log(total)
        lse_ref[0, h : h + 1, :] = jnp.broadcast_to(total_log, (block, 128)).T[:1]


def attend(packed, heads, block, places, count):
    units, length, cols = packed.shape
    wide = heads * HEAD_DIM
    steps = length // block
    return pl.pallas_call(
        functools.partial(attend_kernel, heads, block),
        grid_spec=pltpu.PrefetchScalarGridSpec(
            num_scalar_prefetch=1,
            grid=(units, steps),
            in_specs=[pl.BlockSpec((1, length, cols), lambda u, i, t: (u, 0, 0))],
            out_specs=[
                pl.BlockSpec((1, block, wide), lambda u, i, t: (t[u * steps + i], 0, 0)),
                pl.BlockSpec((1, heads, block), lambda u, i, t: (u, 0, i)),
            ],
            scratch_shapes=[
                pltpu.VMEM((heads, HEAD_DIM, length), BF16),
                pltpu.VMEM((heads, length, 2 * HEAD_DIM), BF16),
            ],
        ),
        out_shape=[
            jax.ShapeDtypeStruct((count, block, wide), BF16),
            jax.ShapeDtypeStruct((units, heads, length), F32),
        ],
        compiler_params=params(),
        cost_estimate=cost(units * heads * 16 * length * length * HEAD_DIM, packed.size * 3, units * heads * length * length),
    )(places, packed)


def attend_back_kernel(
    heads, block, place_ref, x_ref, ctx_ref, dctx_ref, lse_ref, grad_ref, sums_ref, keys_t, keys_s, values_s, dk_s, dv_s
):
    step = pl.program_id(1)

    @pl.when(step == 0)
    def _():
        for h in range(heads):
            c = h * 3 * HEAD_DIM
            key = x_ref[0, :, c + HEAD_DIM : c + 2 * HEAD_DIM]
            keys_s[h] = key
            keys_t[h] = key.T
            values_s[h] = x_ref[0, :, c + 2 * HEAD_DIM : c + 3 * HEAD_DIM]
        dk_s[...] = jnp.zeros_like(dk_s)
        dv_s[...] = jnp.zeros_like(dv_s)

    rows = pl.ds(pl.multiple_of(step * block, block), block)
    here = x_ref[0, rows, :]
    grads = dctx_ref[0]
    prods = ctx_ref[0].astype(F32) * grads.astype(F32)
    for h in range(heads):
        c = h * 3 * HEAD_DIM
        part = slice(h * HEAD_DIM, (h + 1) * HEAD_DIM)
        query = here[:, c : c + HEAD_DIM] * jnp.asarray(HEAD_DIM**-0.5, BF16)
        grad = grads[:, part]
        centre = jnp.sum(prods[:, part].T, 0, keepdims=True)
        scores_t = mm(keys_s[h], query.T)
        probs_t = jnp.exp(scores_t - lse_ref[0, h : h + 1, :])
        grad_probs_t = mm(values_s[h], grad.T)
        grad_scores_t = (probs_t * (grad_probs_t - centre)).astype(BF16)
        dv_s[h] += mm(probs_t.astype(BF16), grad)
        dk_s[h] += mm(grad_scores_t, query)
        grad_query_t = mm(keys_t[h], grad_scores_t)
        grad_ref[0, rows, c : c + HEAD_DIM] = (grad_query_t.T * HEAD_DIM**-0.5).astype(BF16)

    @pl.when(step == pl.num_programs(1) - 1)
    def _():
        for h in range(heads):
            c = h * 3 * HEAD_DIM
            grad_ref[0, :, c + HEAD_DIM : c + 2 * HEAD_DIM] = dk_s[h].astype(BF16)
            grad_ref[0, :, c + 2 * HEAD_DIM : c + 3 * HEAD_DIM] = dv_s[h].astype(BF16)
        sums_ref[0] = jnp.sum(grad_ref[0].astype(F32), 0, keepdims=True)


def attend_back(packed, context, grad_context, lse, heads, block, places):
    units, length, cols = packed.shape
    wide = heads * HEAD_DIM
    steps = length // block
    return pl.pallas_call(
        functools.partial(attend_back_kernel, heads, block),
        grid_spec=pltpu.PrefetchScalarGridSpec(
            num_scalar_prefetch=1,
            grid=(units, steps),
            in_specs=[
                pl.BlockSpec((1, length, cols), lambda u, i, t: (u, 0, 0)),
                pl.BlockSpec((1, block, wide), lambda u, i, t: (t[u * steps + i], 0, 0)),
                pl.BlockSpec((1, block, wide), lambda u, i, t: (t[u * steps + i], 0, 0)),
                pl.BlockSpec((1, heads, block), lambda u, i, t: (u, 0, i)),
            ],
            out_specs=[
                pl.BlockSpec((1, length, cols), lambda u, i, t: (u, 0, 0)),
                pl.BlockSpec((1, 1, cols), lambda u, i, t: (u, 0, 0)),
            ],
            scratch_shapes=[
                pltpu.VMEM((heads, HEAD_DIM, length), BF16),
                pltpu.VMEM((heads, length, HEAD_DIM), BF16),
                pltpu.VMEM((heads, length, HEAD_DIM), BF16),
                pltpu.VMEM((heads, length, HEAD_DIM), F32),
                pltpu.VMEM((heads, length, HEAD_DIM), F32),
            ],
        ),
        out_shape=[
            jax.ShapeDtypeStruct((units, length, cols), BF16),
            jax.ShapeDtypeStruct((units, 1, cols), F32),
        ],
        compiler_params=params(),
        cost_estimate=cost(units * heads * 40 * length * length * HEAD_DIM, packed.size * 5, units * heads * length * length),
    )(places, packed, context, grad_context, lse)


def feed_kernel(
    parts, x_ref, g_ref, widen_ref, narrow_ref, bias_ref, out_ref, dx_ref, grads_ref, bias_grad_ref, out_s, dx_s
):
    step = pl.program_id(0)
    count, depth, tile = widen_ref.shape[1:]
    width = count * depth
    piece = depth // parts
    widen = widen_ref[0].reshape(width, tile)
    normed = x_ref[...]
    grad = g_ref[...]
    narrow = [
        narrow_ref[0, :, c * piece : (c + 1) * piece, :].reshape(tile, tile) for c in range(parts)
    ]
    narrow = jnp.concatenate(narrow, 1)
    bias = jnp.sum(bias_ref[0, 0, 0:3, :].astype(F32), 0, keepdims=True)
    pre = mm(normed, widen) + bias
    cumulative, slope = gelu_parts(pre)
    hidden = (pre * cumulative).astype(BF16)
    grad_pre = (mm(grad, narrow, NT) * (cumulative + slope)).astype(BF16)
    out = mm(hidden, narrow)
    dx = mm(grad_pre, widen, NT)

    @pl.when(step == 0)
    def _():
        out_s[...] = out
        dx_s[...] = dx

    @pl.when(step > 0)
    def _():
        out_s[...] += out
        dx_s[...] += dx

    grads_ref[0, :, :piece, :] = mm(grad_pre, normed, TN).astype(BF16).reshape(count, tile // count, width)
    grads_ref[0, :, piece:, :] = mm(hidden, grad, TN).astype(BF16).reshape(count, tile // count, width)
    bias_grad_ref[0] = jnp.sum(grad_pre.astype(F32), 0, keepdims=True)

    @pl.when(step == pl.num_programs(0) - 1)
    def _():
        out_ref[...] = out_s[...]
        dx_ref[...] = dx_s[...]


def feed(normed, grad, rest, bias_at, extra):
    shards, count, _, tile = rest.shape
    rows, width = normed.shape
    depth = width // count
    parts = width // tile
    piece = tile // count
    return pl.pallas_call(
        functools.partial(feed_kernel, parts),
        grid=(shards,),
        in_specs=[
            pl.BlockSpec((rows, width), lambda m: (0, 0)),
            pl.BlockSpec((rows, width), lambda m: (0, 0)),
            pl.BlockSpec((1, count, depth, tile), lambda m: (m, 0, 0, 0)),
            pl.BlockSpec((1, count, depth, tile), lambda m: (m, 0, 1, 0)),
            pl.BlockSpec((1, 1, 16, tile), lambda m: (m, 0, bias_at // 16, 0)),
        ],
        out_specs=[
            pl.BlockSpec((rows, width), lambda m: (0, 0)),
            pl.BlockSpec((rows, width), lambda m: (0, 0)),
            pl.BlockSpec((1, count, 2 * piece, width), lambda m: (m, 0, 0, 0)),
            pl.BlockSpec((1, 1, tile), lambda m: (m, 0, 0)),
        ],
        out_shape=[
            jax.ShapeDtypeStruct((rows, width), F32),
            jax.ShapeDtypeStruct((rows, width), F32),
            jax.ShapeDtypeStruct((shards, count, 2 * piece + extra, width), BF16),
            jax.ShapeDtypeStruct((shards, 1, tile), F32),
        ],
        scratch_shapes=[pltpu.VMEM((rows, width), F32), pltpu.VMEM((rows, width), F32)],
        compiler_params=params(),
        cost_estimate=cost(12 * shards * rows * width * tile, rest.size * 4 + rows * width * 12, rows * shards * tile),
    )(normed, grad, rest, rest, rest)


def merge_kernel(shards, slots, place_ref, got_ref, w_ref, start_ref, vec_ref, ctx_ref, middle_ref, normed_ref):
    b = pl.program_id(0)
    wide = got_ref.shape[-1]
    for p in range(shards):
        ctx_ref[:, p * wide : (p + 1) * wide] = got_ref[place_ref[b * shards + p]]
    middle = start_ref[...] + mm(ctx_ref[...], w_ref[...]) + vec_ref[0:1, :]
    middle_ref[...] = middle
    normal, _ = norm_parts(middle)
    normed_ref[...] = (normal * vec_ref[1:2, :] + vec_ref[2:3, :]).astype(BF16)


def merge(got, weight, start, vectors, places, slots):
    count, block, wide = got.shape
    rows, width = start.shape
    shards = width // wide
    row_spec = pl.BlockSpec((block, width), lambda b, t: (b, 0))
    return pl.pallas_call(
        functools.partial(merge_kernel, shards, slots),
        grid_spec=pltpu.PrefetchScalarGridSpec(
            num_scalar_prefetch=1,
            grid=(slots,),
            in_specs=[
                pl.BlockSpec(got.shape, lambda b, t: (0, 0, 0)),
                pl.BlockSpec(weight.shape, lambda b, t: (0, 0)),
                row_spec,
                pl.BlockSpec(vectors.shape, lambda b, t: (0, 0)),
            ],
            out_specs=[row_spec, row_spec, row_spec],
        ),
        out_shape=[
            jax.ShapeDtypeStruct((rows, width), BF16),
            jax.ShapeDtypeStruct((rows, width), F32),
            jax.ShapeDtypeStruct((rows, width), BF16),
        ],
        compiler_params=params(),
        cost_estimate=cost(2 * rows * width * width, rows * width * 20),
    )(places, got, weight, start, vectors)


def merge_back_kernel(shards, count, shard_ref, g_ref, w_ref, out_ref, dctx_s):
    wide = out_ref.shape[-1]
    grad = g_ref[...]
    for p in range(shards):
        dctx_s[p] = mm(grad, w_ref[p * wide : (p + 1) * wide, :], NT).astype(BF16)
    for i in range(count):
        out_ref[i] = dctx_s[shard_ref[i]]


def merge_back(grad, weight, shard_of, wide):
    rows, width = grad.shape
    shards = width // wide
    count = shard_of.shape[0]
    return pl.pallas_call(
        functools.partial(merge_back_kernel, shards, count),
        grid_spec=pltpu.PrefetchScalarGridSpec(
            num_scalar_prefetch=1,
            grid=(1,),
            in_specs=[
                pl.BlockSpec((rows, width), lambda b, t: (0, 0)),
                pl.BlockSpec((width, width), lambda b, t: (0, 0)),
            ],
            out_specs=pl.BlockSpec((count, rows, wide), lambda b, t: (0, 0, 0)),
            scratch_shapes=[pltpu.VMEM((shards, rows, wide), BF16)],
        ),
        out_shape=jax.ShapeDtypeStruct((count, rows, wide), BF16),
        compiler_params=params(),
        cost_estimate=cost(2 * rows * width * width, rows * width * 8),
    )(shard_of, grad, weight)


def norm_parts(value):
    mean = jnp.mean(value, -1, keepdims=True)
    centred = value - mean
    scale = lax.rsqrt(jnp.mean(centred * centred, -1, keepdims=True) + EPSILON)
    return centred * scale, scale


def norm_back(normal, scale, gain, grad):
    grad_x = grad * gain
    mean = jnp.mean(grad_x, -1, keepdims=True)
    along = jnp.mean(grad_x * normal, -1, keepdims=True)
    return (
        (grad_x - mean - normal * along) * scale,
        jnp.sum(grad * normal, 0),
        jnp.sum(grad, 0),
    )


def split_rows(array, count):
    share = array.shape[0] // count
    return lax.dynamic_slice_in_dim(array, lax.axis_index("dp") * share, share, 0)


def on_device(
    tokens,
    cotangent,
    group_items,
    dataset_ids,
    lead_hours,
    set_weights,
    lead_weight,
    lead_shift,
    norm_one_gain,
    norm_one_shift,
    heads_weight,
    heads_bias,
    merge_weight,
    merge_bias,
    norm_two_gain,
    norm_two_shift,
    widen_weight,
    widen_bias,
    narrow_weight,
    narrow_bias,
):
    shards = lax.axis_size("mp")
    copies = lax.axis_size("dp")
    rows_here, width = tokens.shape
    group_rows = rows_here * shards
    slots = dataset_ids.shape[0]
    length = group_rows // slots
    block = rows_here // slots
    cols = heads_weight.shape[1]
    heads_here = cols // (3 * HEAD_DIM)
    wide = heads_here * HEAD_DIM
    tile = widen_weight.shape[1]
    parts = width // tile
    dp_at = lax.axis_index("dp")
    mp_at = lax.axis_index("mp")
    both = ("dp", "mp")

    def attention_device(group, k):
        return (group // 2 * 2 + k % 2) * shards + k // 2 * 2 + group % 2

    def row_device(group, k):
        return group * shards + k

    groups = range(copies)
    spots = range(shards)

    def meet(k_rows, k_unit):
        return any(
            (slots * k_rows + b) // shards == (slots * k_unit + j) // shards
            for b in range(slots)
            for j in range(slots)
        )

    swap = [(row_device(g, k), attention_device(g, k)) for g in groups for k in spots]
    core_swap = [(g, g + 1 - g % 2 * 2) for g in groups]
    reach = max(abs(a // 2 - b // 2) for a in spots for b in spots if meet(a, b))
    shifts = [
        s for s in range(1 - shards, shards) if any(0 <= k + s < shards and meet(k + s, k) for k in spots)
    ]
    lowest = shifts[0]

    def far(step):
        return [
            (k, k + 2 * step)
            for k in spots
            if 0 <= k + 2 * step < shards
            and any(
                meet(k // 2 * 2 + a, (k // 2 + step) * 2 + b) or meet((k // 2 + step) * 2 + b, k // 2 * 2 + a)
                for a in range(2)
                for b in range(2)
            )
        ]

    steps = [o for o in range(-reach, reach + 1) if o != 0]

    k_here = mp_at // 2 * 2 + dp_at % 2
    unit_ids = slots * k_here + jnp.arange(slots, dtype=jnp.int32)
    unit_items = unit_ids // shards
    offsets = jnp.arange(-reach, reach + 1, dtype=jnp.int32)
    pair_at = mp_at // 2 + offsets
    core_at = jnp.stack([dp_at % 2, 1 - dp_at % 2]).astype(jnp.int32)
    seen = (pair_at[None, :] * 2 + core_at[:, None])[:, :, None] * slots + jnp.arange(slots, dtype=jnp.int32)
    seen_ok = jnp.broadcast_to(((pair_at >= 0) & (pair_at < shards // 2))[None, :, None], seen.shape)
    table = jnp.concatenate(
        [
            jnp.where(seen_ok, seen // shards, -1).reshape(-1),
            jnp.where(seen_ok, seen % shards, 0).reshape(-1),
            unit_items,
        ]
    ).astype(jnp.int32)
    unit_blocks = unit_items[:, None] * shards + jnp.arange(shards, dtype=jnp.int32)[None, :]
    unit_places = (
        ((unit_blocks // slots - k_here - lowest) * slots + jnp.arange(slots, dtype=jnp.int32)[:, None]) * slots
        + unit_blocks % slots
    ).reshape(-1)
    row_units = (
        (slots * mp_at + jnp.arange(slots, dtype=jnp.int32)) // shards * shards
    )[:, None] + jnp.arange(shards, dtype=jnp.int32)[None, :]
    row_places = (
        ((mp_at - row_units // slots - lowest) * slots + row_units % slots) * slots
        + jnp.arange(slots, dtype=jnp.int32)[:, None]
    ).reshape(-1)
    ends = mp_at - jnp.asarray(shifts, jnp.int32)
    wanted = ((slots * ends[:, None] + jnp.arange(slots, dtype=jnp.int32)[None, :]) % shards).reshape(-1)

    def shift_pairs(s):
        return [
            (attention_device(g, k), row_device(g, k + s))
            for g in groups
            for k in spots
            if 0 <= k + s < shards and meet(k + s, k)
        ]

    def weight_pairs(j):
        return [
            (g * shards + (slots * k + j) % shards, attention_device(g, k)) for g in groups for k in spots
        ]

    def back(pairs):
        return [(b, a) for a, b in pairs]

    row_ids = mp_at * rows_here + jnp.arange(rows_here, dtype=jnp.int32)
    slot_ids = jnp.arange(slots, dtype=jnp.int32)
    slot_table = ((row_ids // length)[:, None] == slot_ids[None, :]).astype(F32)
    lead_scaled = jnp.sum(slot_table * (lead_hours.astype(F32) / 100.0)[None, :], 1)
    live = (slot_ids < group_items[0]).astype(F32)
    set_ids = jnp.arange(set_weights.shape[0], dtype=jnp.int32)
    set_match = (dataset_ids[:, None] == set_ids[None, :]).astype(F32)
    item_weight = live * jnp.sum(set_match * set_weights[None, :], 1)
    row_weight = jnp.sum(slot_table * item_weight[None, :], 1)
    item_total = lax.psum(group_items.astype(F32)[0], "dp")

    start_state = tokens + lead_scaled[:, None] * lead_weight + lead_shift
    first_normal, first_scale = norm_parts(start_state)
    normed_one = (first_normal * norm_one_gain + norm_one_shift).astype(BF16)

    def exact_rows(vector):
        high = vector.astype(BF16)
        left = vector - high.astype(F32)
        middle = left.astype(BF16)
        low = (left - middle.astype(F32)).astype(BF16)
        return jnp.pad(jnp.stack([high, middle, low]), ((0, 13), (0, 0)))

    bias_heads = heads_bias.reshape(heads_here, 2, HEAD_DIM)
    full_bias = jnp.stack(
        [bias_heads[:, 0], jnp.zeros_like(bias_heads[:, 0]), bias_heads[:, 1]], 1
    ).reshape(-1)
    heads_rows = jnp.concatenate([heads_weight, exact_rows(full_bias)], 0)
    unit_weights = jnp.stack([lax.ppermute(heads_rows, both, weight_pairs(j)) for j in range(slots)])

    def fold(part):
        return jnp.concatenate(jnp.split(part, parts, 1), 0)

    rest = jnp.concatenate(
        [
            split_rows(widen_weight, copies),
            fold(split_rows(narrow_weight, copies)),
            fold(split_rows(merge_weight, copies)),
            exact_rows(widen_bias),
        ],
        0,
    )
    merge_rows = merge_weight.shape[0] // copies
    merge_at = 2 * (width // copies)
    bias_at = merge_at + merge_rows * parts

    mine = lax.ppermute(normed_one, both, swap)
    around = {o: lax.ppermute(mine, "mp", far(-o)) for o in steps}
    around[0] = mine
    own = jnp.stack([around[o] for o in range(-reach, reach + 1)])
    own, rest = lax.optimization_barrier((own, rest))
    rest = lax.all_gather(rest, BOTH, axis=0, tiled=True)
    rest = rest.reshape(shards, copies, -1, tile)
    other = lax.ppermute(own, "dp", core_swap).reshape(-1, block, width)
    own = own.reshape(-1, block, width)

    packed = project(own, other, unit_weights, table, length)
    messages = len(shifts) * slots * slots
    context, lse = attend(packed, heads_here, block, unit_places, messages)
    context_out = context.reshape(len(shifts), slots * slots * block, wide)
    context_got = jnp.stack(
        [lax.ppermute(context_out[i], both, shift_pairs(s)) for i, s in enumerate(shifts)]
    ).reshape(messages, block, wide)
    merge_all = rest[:, :, merge_at:bias_at, :].reshape(shards, copies, parts, merge_rows, tile)
    merge_all = merge_all.transpose(0, 1, 3, 2, 4).reshape(width, width)
    merge_vectors = jnp.pad(jnp.stack([merge_bias, norm_two_gain, norm_two_shift]), ((0, 5), (0, 0)))
    context_rows, middle, normed_two = merge(
        context_got, merge_all, start_state, merge_vectors, row_places, slots
    )
    second_normal, second_scale = norm_parts(middle)

    grad_out = cotangent * row_weight[:, None]
    grad_low = grad_out.astype(BF16)
    narrow_bias_grad = jnp.sum(grad_low.astype(F32), 0)
    fed, grad_norm_two, grads_one, widen_bias_grad = feed(normed_two, grad_low, rest, bias_at, merge_rows)
    activations = middle + fed + narrow_bias
    grad_mid_norm, norm_two_gain_grad, norm_two_shift_grad = norm_back(
        second_normal, second_scale, norm_two_gain, grad_norm_two
    )
    grad_middle = grad_out + grad_mid_norm
    grad_mid_low = grad_middle.astype(BF16)
    merge_bias_grad = jnp.sum(grad_mid_low.astype(F32), 0)
    merge_weight_grad = mm(context_rows, grad_mid_low, TN).astype(BF16)
    grads_one = grads_one.at[:, :, -merge_rows:].set(
        merge_weight_grad.reshape(shards, copies, merge_rows, width)
    )
    grads_one = lax.psum_scatter(
        grads_one.reshape(-1, width), BOTH, scatter_dimension=0, tiled=True
    )
    grad_context = merge_back(grad_mid_low, merge_all, wanted, wide).reshape(
        len(shifts), slots * rows_here, wide
    )
    grad_context = jnp.stack(
        [lax.ppermute(grad_context[i], both, back(shift_pairs(s))) for i, s in enumerate(shifts)]
    ).reshape(messages, block, wide)
    grad_packed, unit_sums = attend_back(
        packed, context, grad_context, lse, heads_here, block, unit_places
    )
    own_dx, other_dx, unit_grads = project_back(own, other, unit_weights, grad_packed, table)

    spans = 2 * reach + 1
    other_dx = lax.ppermute(other_dx.reshape(spans, rows_here, width), "dp", core_swap)
    pair_dx = own_dx.reshape(spans, rows_here, width).astype(F32) + other_dx.astype(F32)
    mine_dx = pair_dx[reach]
    for o in steps:
        mine_dx += lax.ppermute(pair_dx[reach + o].astype(BF16), "mp", far(o)).astype(F32)
    grad_norm_one = lax.ppermute(mine_dx.astype(BF16), both, back(swap)).astype(F32)

    heads_total = sum(
        lax.ppermute(unit_grads[j], both, back(weight_pairs(j))).astype(F32) for j in range(slots)
    )
    heads_total = lax.psum(heads_total.astype(BF16), "dp").astype(F32)
    heads_bias_grad = jnp.sum(
        jnp.where(
            (unit_ids % shards)[:, None, None] == jnp.arange(shards, dtype=jnp.int32)[None, :, None],
            unit_sums,
            0.0,
        ),
        0,
    )

    grad_start_norm, norm_one_gain_grad, norm_one_shift_grad = norm_back(
        first_normal, first_scale, norm_one_gain, grad_norm_one
    )
    grad_start = grad_middle + grad_start_norm
    lead_weight_grad = jnp.sum(grad_start * lead_scaled[:, None], 0)
    lead_shift_grad = jnp.sum(grad_start, 0)
    vectors = (
        lead_weight_grad,
        lead_shift_grad,
        norm_one_gain_grad,
        norm_one_shift_grad,
        merge_bias_grad,
        norm_two_gain_grad,
        norm_two_shift_grad,
        narrow_bias_grad,
    )
    vectors = jnp.concatenate(
        [jnp.stack(vectors).reshape(-1), widen_bias_grad.reshape(-1), heads_bias_grad.reshape(-1)]
    )
    vectors = lax.psum(vectors, ("dp", "mp")) / item_total
    shared = vectors[: 8 * width].reshape(8, width)
    place = lax.axis_index("mp")
    widen_bias_total = lax.dynamic_slice_in_dim(vectors, 8 * width + place * tile, tile, 0)
    heads_bias_total = lax.dynamic_slice_in_dim(
        vectors, 8 * width + shards * tile + place * cols, cols, 0
    ).reshape(heads_here, 3, HEAD_DIM)
    heads_bias_total = jnp.stack([heads_bias_total[:, 0], heads_bias_total[:, 2]], 1).reshape(-1)

    grads_one = lax.all_gather(grads_one, "dp", axis=0, tiled=True).astype(F32) / item_total
    grads_one = grads_one.reshape(copies, -1, width)
    piece = tile // copies
    widen_total = grads_one[:, :piece].reshape(tile, width).T
    narrow_total = grads_one[:, piece : 2 * piece].reshape(tile, width)
    merge_total = grads_one[:, 2 * piece :].reshape(-1, width)
    heads_total = heads_total.T / item_total
    return (
        activations,
        grad_start / item_total,
        shared[0],
        shared[1],
        shared[2],
        shared[3],
        heads_total,
        heads_bias_total,
        merge_total,
        shared[4],
        shared[5],
        shared[6],
        widen_total,
        widen_bias_total,
        narrow_total,
        shared[7],
    )


def solution(mesh):
    return jax.shard_map(
        on_device,
        mesh=mesh,
        in_specs=(
            P(("dp", "mp"), None),
            P(("dp", "mp"), None),
            P("dp"),
            P("dp"),
            P("dp"),
            P(),
            P(),
            P(),
            P(),
            P(),
            P(None, "mp"),
            P("mp"),
            P("mp", None),
            P(),
            P(),
            P(),
            P(None, "mp"),
            P("mp"),
            P("mp", None),
            P(),
        ),
        out_specs=(
            P(("dp", "mp"), None),
            P(("dp", "mp"), None),
            P(),
            P(),
            P(),
            P(),
            P(None, "mp"),
            P("mp"),
            P("mp", None),
            P(),
            P(),
            P(),
            P(None, "mp"),
            P("mp"),
            P("mp", None),
            P(),
        ),
        check_vma=False,
    )
```

```python
import functools

import jax
import jax.numpy as jnp
from jax import lax
from jax.experimental import pallas as pl
from jax.experimental.pallas import tpu as pltpu
from jax.sharding import PartitionSpec as P

HEAD_DIM = 64
EPSILON = 1e-05
F32 = jnp.float32
BF16 = jnp.bfloat16
NN = (((1,), (0,)), ((), ()))
NT = (((1,), (1,)), ((), ()))
TN = (((0,), (0,)), ((), ()))
BOTH = ("mp", "dp")
VMEM_LIMIT = 56 * 2**20

TAIL_STEP = 0.35
TAIL = (
    0.13962124730886327,
    0.1398645225480897,
    0.11981419159397333,
    0.10557980057214614,
    -0.023275300634317965,
    0.1594091170984717,
    -0.25591569617440285,
    0.14406734292143564,
    -0.029165241243977125,
)


def mm(left, right, dims=NN):
    return lax.dot_general(left, right, dims, preferred_element_type=F32)


def params():
    return pltpu.CompilerParams(vmem_limit_bytes=VMEM_LIMIT)


def cost(flops, moved, exps=0):
    return pl.CostEstimate(flops=int(flops), bytes_accessed=int(moved), transcendentals=int(exps))


def gelu_parts(value):
    size = jnp.abs(value)
    t = 1.0 / (1.0 + TAIL_STEP * size)
    poly = jnp.full_like(t, TAIL[-1])
    for term in TAIL[-2::-1]:
        poly = poly * t + term
    bell = jnp.exp(-0.5 * value * value)
    tail = poly * t * bell
    cumulative = jnp.where(value >= 0.0, 1.0 - tail, tail)
    return cumulative, value * (bell * 0.3989422804014327)


def collect(items_s, pieces, table_ref, base, shards):
    block = pieces[0].shape[1]
    for i in range(shards):
        for at, piece in enumerate(pieces):

            @pl.when(table_ref[base + 2 * i] == at)
            def _():
                items_s[i * block : (i + 1) * block, :] = piece[table_ref[base + 2 * i + 1]]


def project_kernel(shards, count, table_ref, w_ref, *refs):
    pieces, out_ref, items_s = refs[:count], refs[count], refs[count + 1]
    step = pl.program_id(0)
    width = items_s.shape[1]
    collect(items_s, pieces, table_ref, step * 2 * shards, shards)
    bias = jnp.sum(w_ref[0, width : width + 3, :].astype(F32), 0, keepdims=True)
    out_ref[0] = (mm(items_s[...], w_ref[0, :width, :]) + bias).astype(BF16)


def whole(shape):
    return pl.BlockSpec(shape, lambda *_: (0,) * len(shape))


def project(pieces, weight, table, length, slots):
    shards, depth, cols = weight.shape
    width = pieces[0].shape[2]
    at = 2 * shards * slots + slots
    return pl.pallas_call(
        functools.partial(project_kernel, shards, len(pieces)),
        grid_spec=pltpu.PrefetchScalarGridSpec(
            num_scalar_prefetch=1,
            grid=(slots,),
            in_specs=[pl.BlockSpec((1, depth, cols), lambda j, t: (t[at + j], 0, 0))]
            + [whole(piece.shape) for piece in pieces],
            out_specs=pl.BlockSpec((1, length, cols), lambda j, t: (j, 0, 0)),
            scratch_shapes=[pltpu.VMEM((length, width), BF16)],
        ),
        out_shape=jax.ShapeDtypeStruct((slots, length, cols), BF16),
        compiler_params=params(),
        cost_estimate=cost(2 * slots * length * width * cols, len(pieces) * pieces[0].size * 2 + slots * length * cols * 2),
    )(table, weight, *pieces)


def weight_back_kernel(shards, count, table_ref, g_ref, *refs):
    pieces, out_ref, items_s = refs[:count], refs[count], refs[count + 1]
    collect(items_s, pieces, table_ref, pl.program_id(0) * 2 * shards, shards)
    out_ref[0] = mm(g_ref[0], items_s[...], TN).astype(BF16)


def weight_back(pieces, grad, table):
    slots, length, cols = grad.shape
    width = pieces[0].shape[2]
    shards = length // pieces[0].shape[1]
    return pl.pallas_call(
        functools.partial(weight_back_kernel, shards, len(pieces)),
        grid_spec=pltpu.PrefetchScalarGridSpec(
            num_scalar_prefetch=1,
            grid=(slots,),
            in_specs=[pl.BlockSpec((1, length, cols), lambda j, t: (j, 0, 0))]
            + [whole(piece.shape) for piece in pieces],
            out_specs=pl.BlockSpec((1, cols, width), lambda j, t: (j, 0, 0)),
            scratch_shapes=[pltpu.VMEM((length, width), BF16)],
        ),
        out_shape=jax.ShapeDtypeStruct((slots, cols, width), BF16),
        compiler_params=params(),
        cost_estimate=cost(2 * slots * length * width * cols, len(pieces) * pieces[0].size * 2 + slots * cols * width * 2),
    )(table, grad, *pieces)


def rows_back_kernel(shards, slots, count, table_ref, w_ref, g_ref, *refs):
    outs, sum_s = refs[:count], refs[count]
    block, width = outs[0].shape[1:]
    step = pl.program_id(0)
    tail = 2 * shards * slots + step
    first = jnp.logical_or(step == 0, table_ref[tail] != table_ref[jnp.maximum(tail - 1, 0)])
    last = jnp.logical_or(
        step == slots - 1, table_ref[tail] != table_ref[jnp.minimum(tail + 1, 2 * shards * slots + slots - 1)]
    )

    @pl.when(step == 0)
    def _():
        for out in outs:
            out[...] = jnp.zeros_like(out)

    part = mm(g_ref[0], w_ref[0, :width, :], NT)

    @pl.when(first)
    def _():
        sum_s[...] = part

    @pl.when(jnp.logical_not(first))
    def _():
        sum_s[...] += part

    @pl.when(last)
    def _():
        for i in range(shards):
            base = step * 2 * shards + 2 * i
            for at, out in enumerate(outs):

                @pl.when(table_ref[base] == at)
                def _():
                    out[table_ref[base + 1]] = sum_s[i * block : (i + 1) * block, :].astype(BF16)


def rows_back(grad, weight, table, block, count, blocks, width):
    shards, depth, cols = weight.shape
    slots, length = grad.shape[:2]
    at = 2 * shards * slots + slots
    piece = (blocks, block, width)
    return pl.pallas_call(
        functools.partial(rows_back_kernel, shards, slots, count),
        grid_spec=pltpu.PrefetchScalarGridSpec(
            num_scalar_prefetch=1,
            grid=(slots,),
            in_specs=[
                pl.BlockSpec((1, depth, cols), lambda j, t: (t[at + j], 0, 0)),
                pl.BlockSpec((1, length, cols), lambda j, t: (j, 0, 0)),
            ],
            out_specs=[whole(piece)] * count,
            scratch_shapes=[pltpu.VMEM((length, width), F32)],
        ),
        out_shape=[jax.ShapeDtypeStruct(piece, BF16)] * count,
        compiler_params=params(),
        cost_estimate=cost(2 * slots * length * width * cols, count * blocks * block * width * 2 + grad.size * 2),
    )(table, weight, grad)


def attend_kernel(heads, block, place_ref, x_ref, ctx_ref, lse_ref, keys_s, values_s):
    step = pl.program_id(1)
    length = x_ref.shape[1]

    @pl.when(step == 0)
    def _():
        for h in range(heads):
            c = h * 3 * HEAD_DIM
            keys_s[h] = x_ref[0, :, c + HEAD_DIM : c + 2 * HEAD_DIM].T
            values_s[h, :, :HEAD_DIM] = x_ref[0, :, c + 2 * HEAD_DIM : c + 3 * HEAD_DIM]
            values_s[h, :, HEAD_DIM:] = jnp.ones((length, HEAD_DIM), BF16)

    rows = pl.ds(pl.multiple_of(step * block, block), block)
    here = x_ref[0, rows, :]
    for h in range(heads):
        c = h * 3 * HEAD_DIM
        query = here[:, c : c + HEAD_DIM] * jnp.asarray(HEAD_DIM**-0.5, BF16)
        scores = mm(query, keys_s[h])
        row_max = jnp.max(scores, 1, keepdims=True)
        probs = jnp.exp(scores - row_max).astype(BF16)
        summed = mm(probs, values_s[h])
        total = summed[:, HEAD_DIM : HEAD_DIM + 1]
        ctx_ref[0, :, h * HEAD_DIM : (h + 1) * HEAD_DIM] = (summed[:, :HEAD_DIM] / total).astype(BF16)
        total_log = row_max + jnp.log(total)
        lse_ref[0, h : h + 1, :] = jnp.broadcast_to(total_log, (block, 128)).T[:1]


def attend(packed, heads, block, places, count):
    units, length, cols = packed.shape
    wide = heads * HEAD_DIM
    steps = length // block
    return pl.pallas_call(
        functools.partial(attend_kernel, heads, block),
        grid_spec=pltpu.PrefetchScalarGridSpec(
            num_scalar_prefetch=1,
            grid=(units, steps),
            in_specs=[pl.BlockSpec((1, length, cols), lambda u, i, t: (u, 0, 0))],
            out_specs=[
                pl.BlockSpec((1, block, wide), lambda u, i, t: (t[u * steps + i], 0, 0)),
                pl.BlockSpec((1, heads, block), lambda u, i, t: (u, 0, i)),
            ],
            scratch_shapes=[
                pltpu.VMEM((heads, HEAD_DIM, length), BF16),
                pltpu.VMEM((heads, length, 2 * HEAD_DIM), BF16),
            ],
        ),
        out_shape=[
            jax.ShapeDtypeStruct((count, block, wide), BF16),
            jax.ShapeDtypeStruct((units, heads, length), F32),
        ],
        compiler_params=params(),
        cost_estimate=cost(units * heads * 16 * length * length * HEAD_DIM, packed.size * 3, units * heads * length * length),
    )(places, packed)


def attend_back_kernel(
    heads, block, place_ref, x_ref, ctx_ref, dctx_ref, lse_ref, grad_ref, sums_ref, keys_t, keys_s, values_s, dk_s, dv_s
):
    step = pl.program_id(1)

    @pl.when(step == 0)
    def _():
        for h in range(heads):
            c = h * 3 * HEAD_DIM
            key = x_ref[0, :, c + HEAD_DIM : c + 2 * HEAD_DIM]
            keys_s[h] = key
            keys_t[h] = key.T
            values_s[h] = x_ref[0, :, c + 2 * HEAD_DIM : c + 3 * HEAD_DIM]
        dk_s[...] = jnp.zeros_like(dk_s)
        dv_s[...] = jnp.zeros_like(dv_s)

    rows = pl.ds(pl.multiple_of(step * block, block), block)
    here = x_ref[0, rows, :]
    grads = dctx_ref[0]
    prods = ctx_ref[0].astype(F32) * grads.astype(F32)
    for h in range(heads):
        c = h * 3 * HEAD_DIM
        part = slice(h * HEAD_DIM, (h + 1) * HEAD_DIM)
        query = here[:, c : c + HEAD_DIM] * jnp.asarray(HEAD_DIM**-0.5, BF16)
        grad = grads[:, part]
        centre = jnp.sum(prods[:, part].T, 0, keepdims=True)
        scores_t = mm(keys_s[h], query.T)
        probs_t = jnp.exp(scores_t - lse_ref[0, h : h + 1, :])
        grad_probs_t = mm(values_s[h], grad.T)
        grad_scores_t = (probs_t * (grad_probs_t - centre)).astype(BF16)
        dv_s[h] += mm(probs_t.astype(BF16), grad)
        dk_s[h] += mm(grad_scores_t, query)
        grad_query_t = mm(keys_t[h], grad_scores_t)
        grad_ref[0, rows, c : c + HEAD_DIM] = (grad_query_t.T * HEAD_DIM**-0.5).astype(BF16)

    @pl.when(step == pl.num_programs(1) - 1)
    def _():
        for h in range(heads):
            c = h * 3 * HEAD_DIM
            grad_ref[0, :, c + HEAD_DIM : c + 2 * HEAD_DIM] = dk_s[h].astype(BF16)
            grad_ref[0, :, c + 2 * HEAD_DIM : c + 3 * HEAD_DIM] = dv_s[h].astype(BF16)
        sums_ref[0] = jnp.sum(grad_ref[0].astype(F32), 0, keepdims=True)


def attend_back(packed, context, grad_context, lse, heads, block, places):
    units, length, cols = packed.shape
    wide = heads * HEAD_DIM
    steps = length // block
    return pl.pallas_call(
        functools.partial(attend_back_kernel, heads, block),
        grid_spec=pltpu.PrefetchScalarGridSpec(
            num_scalar_prefetch=1,
            grid=(units, steps),
            in_specs=[
                pl.BlockSpec((1, length, cols), lambda u, i, t: (u, 0, 0)),
                pl.BlockSpec((1, block, wide), lambda u, i, t: (t[u * steps + i], 0, 0)),
                pl.BlockSpec((1, block, wide), lambda u, i, t: (t[u * steps + i], 0, 0)),
                pl.BlockSpec((1, heads, block), lambda u, i, t: (u, 0, i)),
            ],
            out_specs=[
                pl.BlockSpec((1, length, cols), lambda u, i, t: (u, 0, 0)),
                pl.BlockSpec((1, 1, cols), lambda u, i, t: (u, 0, 0)),
            ],
            scratch_shapes=[
                pltpu.VMEM((heads, HEAD_DIM, length), BF16),
                pltpu.VMEM((heads, length, HEAD_DIM), BF16),
                pltpu.VMEM((heads, length, HEAD_DIM), BF16),
                pltpu.VMEM((heads, length, HEAD_DIM), F32),
                pltpu.VMEM((heads, length, HEAD_DIM), F32),
            ],
        ),
        out_shape=[
            jax.ShapeDtypeStruct((units, length, cols), BF16),
            jax.ShapeDtypeStruct((units, 1, cols), F32),
        ],
        compiler_params=params(),
        cost_estimate=cost(units * heads * 40 * length * length * HEAD_DIM, packed.size * 5, units * heads * length * length),
    )(places, packed, context, grad_context, lse)


def feed_kernel(
    parts, x_ref, g_ref, widen_ref, narrow_ref, bias_ref, out_ref, dx_ref, hidden_ref, pre_ref, bias_grad_ref, out_s, dx_s
):
    step = pl.program_id(0)
    some, count, depth, tile = widen_ref.shape
    piece = depth // parts
    widen = jnp.concatenate([widen_ref[a].reshape(count * depth, tile) for a in range(some)], 1)
    narrow = jnp.concatenate(
        [
            jnp.concatenate(
                [narrow_ref[a, :, c * piece : (c + 1) * piece, :].reshape(tile, tile) for c in range(parts)], 1
            )
            for a in range(some)
        ],
        0,
    )
    bias = jnp.concatenate(
        [jnp.sum(bias_ref[a, 0, 0:3, :].astype(F32), 0, keepdims=True) for a in range(some)], 1
    )
    pre = mm(x_ref[...], widen) + bias
    cumulative, slope = gelu_parts(pre)
    hidden = (pre * cumulative).astype(BF16)
    grad_pre = (mm(g_ref[...], narrow, NT) * (cumulative + slope)).astype(BF16)
    hidden_ref[0] = hidden
    pre_ref[0] = grad_pre
    bias_grad_ref[0] = jnp.sum(grad_pre.astype(F32), 0, keepdims=True)
    out = mm(hidden, narrow)
    dx = mm(grad_pre, widen, NT)

    @pl.when(step == 0)
    def _():
        out_s[...] = out
        dx_s[...] = dx

    @pl.when(step > 0)
    def _():
        out_s[...] += out
        dx_s[...] += dx

    @pl.when(step == pl.num_programs(0) - 1)
    def _():
        out_ref[...] = out_s[...].astype(out_ref.dtype)
        dx_ref[...] = dx_s[...].astype(dx_ref.dtype)


def feed(normed, grad, rest, bias_at, some, dtype):
    shards, count, _, tile = rest.shape
    rows, width = normed.shape
    depth = width // count
    parts = width // tile
    steps = shards // some
    unit_spec = pl.BlockSpec((1, rows, some * tile), lambda m: (m, 0, 0))
    return pl.pallas_call(
        functools.partial(feed_kernel, parts),
        grid=(steps,),
        in_specs=[
            whole((rows, width)),
            whole((rows, width)),
            pl.BlockSpec((some, count, depth, tile), lambda m: (m, 0, 0, 0)),
            pl.BlockSpec((some, count, depth, tile), lambda m: (m, 0, 1, 0)),
            pl.BlockSpec((some, 1, 16, tile), lambda m: (m, 0, bias_at // 16, 0)),
        ],
        out_specs=[
            whole((rows, width)),
            whole((rows, width)),
            unit_spec,
            unit_spec,
            pl.BlockSpec((1, 1, some * tile), lambda m: (m, 0, 0)),
        ],
        out_shape=[
            jax.ShapeDtypeStruct((rows, width), dtype),
            jax.ShapeDtypeStruct((rows, width), dtype),
            jax.ShapeDtypeStruct((steps, rows, some * tile), BF16),
            jax.ShapeDtypeStruct((steps, rows, some * tile), BF16),
            jax.ShapeDtypeStruct((steps, 1, some * tile), F32),
        ],
        scratch_shapes=[pltpu.VMEM((rows, width), F32), pltpu.VMEM((rows, width), F32)],
        compiler_params=params(),
        cost_estimate=cost(8 * shards * rows * width * tile, rest.size * 2 + rows * width * 28, rows * shards * tile),
    )(normed, grad, rest, rest, rest)


def feed_grads_kernel(*refs):
    out_ref = refs[-1]
    some, count, both, width = out_ref.shape
    piece = both // 2
    widen = narrow = 0.0
    for at in range(0, len(refs) - 1, 4):
        x_ref, g_ref, hidden_ref, pre_ref = refs[at : at + 4]
        widen += mm(pre_ref[0], x_ref[...], TN)
        narrow += mm(hidden_ref[0], g_ref[...], TN)
    out_ref[:, :, :piece, :] = widen.astype(BF16).reshape(some, count, piece, width)
    out_ref[:, :, piece:, :] = narrow.astype(BF16).reshape(some, count, piece, width)


def feed_grads(feed_parts, count, some, extra):
    steps, _, tiles = feed_parts[0][2].shape
    width = feed_parts[0][0].shape[1]
    both = 2 * tiles // some // count
    specs, rows_all = [], 0
    for part in feed_parts:
        rows = part[0].shape[0]
        rows_all += rows
        unit_spec = pl.BlockSpec((1, rows, tiles), lambda m: (m, 0, 0))
        specs += [whole((rows, width)), whole((rows, width)), unit_spec, unit_spec]
    return pl.pallas_call(
        feed_grads_kernel,
        grid=(steps,),
        in_specs=specs,
        out_specs=pl.BlockSpec((some, count, both, width), lambda m: (m, 0, 0, 0)),
        out_shape=jax.ShapeDtypeStruct((steps * some, count, both + extra, width), BF16),
        compiler_params=params(),
        cost_estimate=cost(4 * steps * rows_all * width * tiles, steps * rows_all * tiles * 4 + steps * tiles * width * 4),
    )(*[array for part in feed_parts for array in part])


def merge_kernel(shards, slots, place_ref, got_ref, w_ref, start_ref, vec_ref, ctx_ref, middle_ref, normed_ref):
    b = pl.program_id(0)
    wide = got_ref.shape[-1]
    for p in range(shards):
        ctx_ref[:, p * wide : (p + 1) * wide] = got_ref[place_ref[b * shards + p]]
    middle = start_ref[...] + mm(ctx_ref[...], w_ref[...]) + vec_ref[0:1, :]
    middle_ref[...] = middle
    normal, _ = norm_parts(middle)
    normed_ref[...] = (normal * vec_ref[1:2, :] + vec_ref[2:3, :]).astype(BF16)


def merge(got, weight, start, vectors, places, slots):
    count, block, wide = got.shape
    rows, width = start.shape
    shards = width // wide
    row_spec = pl.BlockSpec((block, width), lambda b, t: (b, 0))
    return pl.pallas_call(
        functools.partial(merge_kernel, shards, slots),
        grid_spec=pltpu.PrefetchScalarGridSpec(
            num_scalar_prefetch=1,
            grid=(slots,),
            in_specs=[
                pl.BlockSpec(got.shape, lambda b, t: (0, 0, 0)),
                pl.BlockSpec(weight.shape, lambda b, t: (0, 0)),
                row_spec,
                pl.BlockSpec(vectors.shape, lambda b, t: (0, 0)),
            ],
            out_specs=[row_spec, row_spec, row_spec],
        ),
        out_shape=[
            jax.ShapeDtypeStruct((rows, width), BF16),
            jax.ShapeDtypeStruct((rows, width), F32),
            jax.ShapeDtypeStruct((rows, width), BF16),
        ],
        compiler_params=params(),
        cost_estimate=cost(2 * rows * width * width, rows * width * 20),
    )(places, got, weight, start, vectors)


def merge_back_kernel(shards, count, shard_ref, g_ref, w_ref, out_ref, dctx_s):
    wide = out_ref.shape[-1]
    grad = g_ref[...]
    for p in range(shards):
        dctx_s[p] = mm(grad, w_ref[p * wide : (p + 1) * wide, :], NT).astype(BF16)
    for i in range(count):
        out_ref[i] = dctx_s[shard_ref[i]]


def merge_back(grad, weight, shard_of, wide):
    rows, width = grad.shape
    shards = width // wide
    count = shard_of.shape[0]
    return pl.pallas_call(
        functools.partial(merge_back_kernel, shards, count),
        grid_spec=pltpu.PrefetchScalarGridSpec(
            num_scalar_prefetch=1,
            grid=(1,),
            in_specs=[
                pl.BlockSpec((rows, width), lambda b, t: (0, 0)),
                pl.BlockSpec((width, width), lambda b, t: (0, 0)),
            ],
            out_specs=pl.BlockSpec((count, rows, wide), lambda b, t: (0, 0, 0)),
            scratch_shapes=[pltpu.VMEM((shards, rows, wide), BF16)],
        ),
        out_shape=jax.ShapeDtypeStruct((count, rows, wide), BF16),
        compiler_params=params(),
        cost_estimate=cost(2 * rows * width * width, rows * width * 8),
    )(shard_of, grad, weight)


def norm_parts(value):
    mean = jnp.mean(value, -1, keepdims=True)
    centred = value - mean
    scale = lax.rsqrt(jnp.mean(centred * centred, -1, keepdims=True) + EPSILON)
    return centred * scale, scale


def norm_back(normal, scale, gain, grad):
    grad_x = grad * gain
    mean = jnp.mean(grad_x, -1, keepdims=True)
    along = jnp.mean(grad_x * normal, -1, keepdims=True)
    return (
        (grad_x - mean - normal * along) * scale,
        jnp.sum(grad * normal, 0),
        jnp.sum(grad, 0),
    )


def share_of(array, at, count):
    share = array.shape[0] // count
    return lax.dynamic_slice_in_dim(array, at * share, share, 0)


def on_device(
    tokens,
    cotangent,
    group_items,
    dataset_ids,
    lead_hours,
    set_weights,
    lead_weight,
    lead_shift,
    norm_one_gain,
    norm_one_shift,
    heads_weight,
    heads_bias,
    merge_weight,
    merge_bias,
    norm_two_gain,
    norm_two_shift,
    widen_weight,
    widen_bias,
    narrow_weight,
    narrow_bias,
):
    shards = lax.axis_size("mp")
    copies = lax.axis_size("dp")
    rows_here, width = tokens.shape
    group_rows = rows_here * shards
    slots = dataset_ids.shape[0]
    length = group_rows // slots
    block = rows_here // slots
    cols = heads_weight.shape[1]
    heads_here = cols // (3 * HEAD_DIM)
    wide = heads_here * HEAD_DIM
    tile = widen_weight.shape[1] // 2
    parts = width // tile
    count = copies // 2
    some = 2
    dp_at = lax.axis_index("dp")
    mp_at = lax.axis_index("mp")
    both = ("dp", "mp")

    def attention_device(group, k):
        return (group // 2 * 2 + k % 2) * shards + k // 2 * 2 + group % 2

    def row_device(group, k):
        return group * shards + k

    groups = range(copies)
    spots = range(shards)

    def meet(k_rows, k_unit):
        return any(
            (slots * k_rows + b) // shards == (slots * k_unit + j) // shards
            for b in range(slots)
            for j in range(slots)
        )

    core_swap = [(g, g + 1 - g % 2 * 2) for g in groups]
    half_swap = [(g, g ^ 2) for g in groups]
    half_at = dp_at // 2 % 2
    piece_at = dp_at // 4 * 2 + dp_at % 2
    plane = [[k * copies + g for k in spots for g in groups if g // 2 % 2 == h] for h in range(2)]
    row_swap = [(k, k + 1 - k % 2 * 2) for k in spots]
    reach = max(abs(a // 2 - b // 2) for a in spots for b in spots if meet(a, b))
    classes = []
    for s in sorted(range(1 - shards, shards), key=abs):
        pairs = [(k, k + s) for k in spots if 0 <= k + s < shards and meet(k + s, k)]
        for known in classes:
            if not any(a == c or b == d for a, b in pairs for c, d in known):
                known += pairs
                break
        else:
            if pairs:
                classes.append(pairs)
    color = [[0] * shards for _ in spots]
    senders = [[0] * shards for _ in classes]
    for i, pairs in enumerate(classes):
        for unit, rows in pairs:
            color[unit][rows] = i
            senders[i][rows] = unit
    color = jnp.asarray(color, jnp.int32)
    senders = jnp.asarray(senders, jnp.int32)

    def extents(pairs):
        ranges = []
        for unit, rows in pairs:
            shared = [
                (j, b)
                for j in range(slots)
                for b in range(slots)
                if (slots * rows + b) // shards == (slots * unit + j) // shards
            ]
            ranges.append([(min(part), max(part) + 1) for part in zip(*shared)])
        sizes = [max(r[at][1] - r[at][0] for r in ranges) for at in range(2)]
        unit_starts = [[0] * shards for _ in range(2)]
        row_starts = [[0] * shards for _ in range(2)]
        for (unit, rows), r in zip(pairs, ranges):
            for at in range(2):
                unit_starts[at][unit] = row_starts[at][rows] = min(r[at][0], slots - sizes[at])
        return sizes, unit_starts, row_starts

    def exchange(array, to_rows):
        got = []
        for i, pairs in enumerate(classes):
            sizes, unit_starts, row_starts = extents(pairs)
            ends = [(attention_device(g, unit), row_device(g, rows)) for g in groups for unit, rows in pairs]
            ends = ends if to_rows else back(ends)
            message = array[i]
            if sizes == [slots, slots]:
                got.append(lax.ppermute(message, both, ends))
                continue
            at_unit = [jnp.asarray(part, jnp.int32)[k_here] for part in unit_starts]
            at_rows = [jnp.asarray(part, jnp.int32)[mp_at] for part in row_starts]
            at_from, at_to = (at_unit, at_rows) if to_rows else (at_rows, at_unit)
            some_part = lax.dynamic_slice(message, (*at_from, 0, 0), (*sizes, *message.shape[2:]))
            some_part = lax.ppermute(some_part, both, ends)
            got.append((some_part, at_to))
        return got

    def together(got, shape):
        whole_ones = [
            lax.dynamic_update_slice(jnp.zeros(shape, BF16), part[0], (*part[1], 0, 0))
            if isinstance(part, tuple)
            else part
            for part in got
        ]
        return jnp.stack(whole_ones).reshape(-1, *shape[2:])

    def far(step):
        return [
            (attention_device(g, k), row_device(g, k + 2 * step))
            for g in groups
            for k in spots
            if 0 <= k + 2 * step < shards and any(meet(k + 2 * step, k // 2 * 2 + b) for b in range(2))
        ]

    def back(pairs):
        return [(b, a) for a, b in pairs]

    steps = range(-reach, reach + 1)

    k_here = mp_at // 2 * 2 + dp_at % 2
    unit_ids = slots * k_here + jnp.arange(slots, dtype=jnp.int32)
    unit_items = unit_ids // shards
    unit_blocks = unit_items[:, None] * shards + jnp.arange(shards, dtype=jnp.int32)[None, :]
    block_spots = unit_blocks // slots
    table = jnp.stack(
        [
            (block_spots + dp_at) % 2,
            (block_spots // 2 - mp_at // 2 + reach) * slots + unit_blocks % slots,
        ],
        2,
    )
    table = jnp.concatenate([table.reshape(-1), unit_items, unit_ids % shards]).astype(jnp.int32)
    counting = jnp.arange(slots, dtype=jnp.int32)
    unit_places = (
        (color[k_here, block_spots] * slots + counting[:, None]) * slots + unit_blocks % slots
    ).reshape(-1)
    row_units = ((slots * mp_at + counting) // shards * shards)[:, None] + jnp.arange(
        shards, dtype=jnp.int32
    )[None, :]
    row_places = (
        (color[row_units // slots, mp_at] * slots + row_units % slots) * slots + counting[:, None]
    ).reshape(-1)
    wanted = ((slots * senders[:, mp_at][:, None] + counting[None, :]) % shards).reshape(-1)

    def weight_pairs(j):
        return [
            (g * shards + (slots * k + j) % shards, attention_device(g, k)) for g in groups for k in spots
        ]

    row_ids = mp_at * rows_here + jnp.arange(rows_here, dtype=jnp.int32)
    slot_ids = jnp.arange(slots, dtype=jnp.int32)
    slot_table = ((row_ids // length)[:, None] == slot_ids[None, :]).astype(F32)
    lead_scaled = jnp.sum(slot_table * (lead_hours.astype(F32) / 100.0)[None, :], 1)
    live = (slot_ids < group_items[0]).astype(F32)
    set_ids = jnp.arange(set_weights.shape[0], dtype=jnp.int32)
    set_match = (dataset_ids[:, None] == set_ids[None, :]).astype(F32)
    item_weight = live * jnp.sum(set_match * set_weights[None, :], 1)
    row_weight = jnp.sum(slot_table * item_weight[None, :], 1)

    start_state = tokens + lead_scaled[:, None] * lead_weight + lead_shift
    first_normal, first_scale = norm_parts(start_state)
    normed_one = (first_normal * norm_one_gain + norm_one_shift).astype(BF16)

    def exact_rows(vector, pad):
        high = vector.astype(BF16)
        left = vector - high.astype(F32)
        middle = left.astype(BF16)
        low = (left - middle.astype(F32)).astype(BF16)
        return jnp.pad(jnp.stack([high, middle, low]), ((0, pad - 3), (0, 0)))

    bias_heads = heads_bias.reshape(heads_here, 2, HEAD_DIM)
    full_bias = jnp.stack(
        [bias_heads[:, 0], jnp.zeros_like(bias_heads[:, 0]), bias_heads[:, 1]], 1
    ).reshape(-1)
    heads_rows = jnp.concatenate([heads_weight, exact_rows(full_bias, 16 * count)], 0)
    heads_all = lax.all_gather(
        share_of(heads_rows, piece_at, count), BOTH, axis=0, tiled=True, axis_index_groups=plane
    ).reshape(shards, -1, cols)

    def fold(part):
        return jnp.concatenate(jnp.split(part, parts, 1), 0)

    rest = jnp.concatenate(
        [
            share_of(lax.dynamic_slice_in_dim(widen_weight, half_at * tile, tile, 1), piece_at, count),
            fold(share_of(share_of(narrow_weight, half_at, 2), piece_at, count)),
            fold(share_of(merge_weight, piece_at, count)),
            exact_rows(share_of(widen_bias, half_at, 2), 16),
        ],
        0,
    )
    merge_rows = merge_weight.shape[0] // count
    merge_at = 2 * (width // count)
    bias_at = merge_at + merge_rows * parts

    own = jnp.stack([lax.ppermute(normed_one, both, back(far(o))) for o in steps])
    grad_out = cotangent * row_weight[:, None]
    grad_low = grad_out.astype(BF16)
    own, rest, grad_low, live_items = lax.optimization_barrier((own, rest, grad_low, group_items))
    item_total = lax.psum(live_items.astype(F32)[0], "dp")
    rest = lax.all_gather(rest, BOTH, axis=0, tiled=True, axis_index_groups=plane)
    rest = rest.reshape(shards, count, -1, tile)
    their_grad = lax.ppermute(grad_low, "dp", half_swap)
    other = lax.ppermute(own, "dp", core_swap)
    other, item_total = lax.optimization_barrier((other, item_total))
    pieces = [part.reshape(-1, block, width) for part in (own, other)]

    packed = project(pieces, heads_all, table, length, slots)
    messages = len(classes) * slots * slots
    message = (slots, slots, block, wide)
    context, lse = attend(packed, heads_here, block, unit_places, messages)
    context_got = together(exchange(context.reshape(-1, *message), True), message)
    merge_all = rest[:, :, merge_at:bias_at, :].reshape(shards, count, parts, merge_rows, tile)
    merge_all = merge_all.transpose(0, 1, 3, 2, 4).reshape(width, width)
    merge_vectors = jnp.pad(jnp.stack([merge_bias, norm_two_gain, norm_two_shift]), ((0, 5), (0, 0)))
    context_rows, middle, normed_two = merge(
        context_got, merge_all, start_state, merge_vectors, row_places, slots
    )
    second_normal, second_scale = norm_parts(middle)

    narrow_bias_grad = jnp.sum(grad_low.astype(F32), 0)
    chunk = rows_here // 2
    chunks = [slice(0, chunk), slice(chunk, rows_here)]
    their_normed = [lax.ppermute(normed_two[rows], "dp", half_swap) for rows in chunks]
    fed, grad_norm_two, hidden, grad_pre, widen_bias_grad = feed(
        normed_two, grad_low, rest, bias_at, some, F32
    )
    feed_parts = [(normed_two, grad_low, hidden, grad_pre)]
    their_fed, their_dx = [], []
    for i, rows in enumerate(chunks):
        their_normed[i], fed = lax.optimization_barrier((their_normed[i], fed))
        their = (their_normed[i], their_grad[rows])
        part_fed, part_dx, hidden, grad_pre, part_bias = feed(*their, rest, bias_at, some, BF16)
        feed_parts.append(their + (hidden, grad_pre))
        widen_bias_grad += part_bias
        their_fed.append(part_fed)
        their_dx.append(lax.ppermute(part_dx, "dp", half_swap))
        fed = lax.optimization_barrier((fed, part_dx))[0]
    their_dx[-1], *their_fed = lax.optimization_barrier((their_dx[-1], *their_fed))
    grad_norm_two = grad_norm_two + jnp.concatenate(their_dx).astype(F32)
    their_fed = lax.ppermute(jnp.concatenate(their_fed), "dp", half_swap)
    widen_bias_grad = widen_bias_grad.reshape(shards, 1, tile)
    widen_bias_grad = jnp.where(
        jnp.arange(2, dtype=jnp.int32)[None, :, None] == half_at, widen_bias_grad, 0.0
    )
    grad_mid_norm, norm_two_gain_grad, norm_two_shift_grad = norm_back(
        second_normal, second_scale, norm_two_gain, grad_norm_two
    )
    grad_middle = grad_out + grad_mid_norm
    grad_mid_low = grad_middle.astype(BF16)
    merge_bias_grad = jnp.sum(grad_mid_low.astype(F32), 0)
    grad_context = merge_back(grad_mid_low, merge_all, wanted, wide)
    grad_context = exchange(grad_context.reshape(-1, *message), False)
    first = feed_parts[0][:2]
    grad_context[0], *hold = lax.optimization_barrier((grad_context[0], *feed_parts[0][2:]))
    feed_parts[0] = first + tuple(hold)
    grads_one = feed_grads(feed_parts, count, some, merge_weight.shape[0] // copies)
    grad_context[1], grads_one = lax.optimization_barrier((grad_context[1], grads_one))
    grad_context = together(grad_context, message)
    merge_weight_grad = mm(context_rows, grad_mid_low, TN).astype(BF16)
    merge_weight_grad = merge_weight_grad.reshape(shards, copies // 4, 2, 2, -1, width)
    kept = lax.dynamic_index_in_dim(merge_weight_grad, half_at, 2, False)
    sent = lax.dynamic_index_in_dim(merge_weight_grad, 1 - half_at, 2, False)
    kept = kept.astype(F32) + lax.ppermute(sent, "dp", half_swap).astype(F32)
    grads_one = grads_one.at[:, :, 2 * (tile // count) :].set(
        kept.astype(BF16).reshape(shards, count, -1, width)
    )
    grads_one = lax.psum_scatter(
        grads_one.reshape(-1, width), BOTH, scatter_dimension=0, tiled=True, axis_index_groups=plane
    )
    grad_packed, unit_sums = attend_back(
        packed, context, grad_context, lse, heads_here, block, unit_places
    )
    grad_packed, their_fed = lax.optimization_barrier((grad_packed, their_fed))
    activations = middle + fed + their_fed.astype(F32) + narrow_bias
    own_dx, other_dx = rows_back(grad_packed, heads_all, table, block, 2, len(steps) * slots, width)

    other_dx = lax.ppermute(other_dx, "dp", core_swap).reshape(-1, rows_here, width)
    own_dx = own_dx.reshape(-1, rows_here, width)
    pair_dx = [(own_dx[i].astype(F32) + other_dx[i].astype(F32)).astype(BF16) for i in range(len(steps))]
    grad_packed, *pair_dx = lax.optimization_barrier((grad_packed, *pair_dx))
    grad_norm_one = [lax.ppermute(pair_dx[i], both, far(o)) for i, o in enumerate(steps)]

    unit_grads = weight_back(pieces, grad_packed, table)
    grad_norm_one[-1], unit_grads = lax.optimization_barrier((grad_norm_one[-1], unit_grads))
    grad_norm_one = sum(part.astype(F32) for part in grad_norm_one)
    heads_parts = [lax.ppermute(unit_grads[j], both, back(weight_pairs(j))) for j in range(slots)]
    heads_bias_grad = jnp.sum(
        jnp.where(
            (unit_ids % shards)[:, None, None] == jnp.arange(shards, dtype=jnp.int32)[None, :, None],
            unit_sums,
            0.0,
        ),
        0,
    )

    grad_start_norm, norm_one_gain_grad, norm_one_shift_grad = norm_back(
        first_normal, first_scale, norm_one_gain, grad_norm_one
    )
    grad_start = grad_middle + grad_start_norm
    lead_weight_grad = jnp.sum(grad_start * lead_scaled[:, None], 0)
    lead_shift_grad = jnp.sum(grad_start, 0)
    vectors = (
        lead_weight_grad,
        lead_shift_grad,
        norm_one_gain_grad,
        norm_one_shift_grad,
        merge_bias_grad,
        norm_two_gain_grad,
        norm_two_shift_grad,
        narrow_bias_grad,
    )
    vectors = jnp.concatenate(
        [jnp.stack(vectors).reshape(-1), widen_bias_grad.reshape(-1), heads_bias_grad.reshape(-1)]
    )
    hops = [
        (axis, [(i, i ^ 1 << bit) for i in range(size)])
        for axis, size in (("dp", copies), ("mp", shards))
        for bit in range((size - 1).bit_length())
    ]
    heads_total = None
    for at, (axis, pairs) in enumerate(hops):
        vectors += lax.ppermute(vectors, axis, pairs)
        if at == 0:
            vectors, *heads_parts = lax.optimization_barrier((vectors, *heads_parts))
            heads_total = sum(part.astype(F32) for part in heads_parts).astype(BF16)
        elif at <= (copies - 1).bit_length():
            axis, pairs = hops[at - 1]
            over = lax.ppermute(heads_total, axis, pairs)
            heads_total = (heads_total.astype(F32) + over.astype(F32)).astype(BF16)
    vectors, heads_total = lax.optimization_barrier((vectors / item_total, heads_total))
    heads_total = heads_total.astype(F32)
    shared = vectors[: 8 * width].reshape(8, width)
    place = lax.axis_index("mp")
    widen_bias_total = lax.dynamic_slice_in_dim(vectors, 8 * width + place * 2 * tile, 2 * tile, 0)
    heads_bias_total = lax.dynamic_slice_in_dim(
        vectors, 8 * width + shards * 2 * tile + place * cols, cols, 0
    ).reshape(heads_here, 3, HEAD_DIM)
    heads_bias_total = jnp.stack([heads_bias_total[:, 0], heads_bias_total[:, 2]], 1).reshape(-1)

    grads_one = lax.all_gather(grads_one, "dp", axis=0, tiled=True).astype(F32) / item_total
    piece = tile // count
    grads_one = grads_one.reshape(copies // 4, 2, 2, -1, width).transpose(1, 0, 2, 3, 4)
    widen_total = grads_one[:, :, :, :piece].reshape(2 * tile, width).T
    narrow_total = grads_one[:, :, :, piece : 2 * piece].reshape(2 * tile, width)
    merge_total = grads_one[:, :, :, 2 * piece :].transpose(1, 0, 2, 3, 4).reshape(-1, width)
    heads_total = heads_total.T / item_total
    return (
        activations,
        grad_start / item_total,
        shared[0],
        shared[1],
        shared[2],
        shared[3],
        heads_total,
        heads_bias_total,
        merge_total,
        shared[4],
        shared[5],
        shared[6],
        widen_total,
        widen_bias_total,
        narrow_total,
        shared[7],
    )


def solution(mesh):
    return jax.shard_map(
        on_device,
        mesh=mesh,
        in_specs=(
            P(("dp", "mp"), None),
            P(("dp", "mp"), None),
            P("dp"),
            P("dp"),
            P("dp"),
            P(),
            P(),
            P(),
            P(),
            P(),
            P(None, "mp"),
            P("mp"),
            P("mp", None),
            P(),
            P(),
            P(),
            P(None, "mp"),
            P("mp"),
            P("mp", None),
            P(),
        ),
        out_specs=(
            P(("dp", "mp"), None),
            P(("dp", "mp"), None),
            P(),
            P(),
            P(),
            P(),
            P(None, "mp"),
            P("mp"),
            P("mp", None),
            P(),
            P(),
            P(),
            P(None, "mp"),
            P("mp"),
            P("mp", None),
            P(),
        ),
        check_vma=False,
    )
```

```python
import functools

import jax
import jax.numpy as jnp
from jax import lax
from jax.experimental import pallas as pl
from jax.experimental.pallas import tpu as pltpu
from jax.sharding import PartitionSpec as P

HEAD_DIM = 64
EPSILON = 1e-05
F32 = jnp.float32
BF16 = jnp.bfloat16
NN = (((1,), (0,)), ((), ()))
NT = (((1,), (1,)), ((), ()))
TN = (((0,), (0,)), ((), ()))
BOTH = ("mp", "dp")
VMEM_LIMIT = 56 * 2**20

TAIL_STEP = 0.35
TAIL = (
    0.13962124730886327,
    0.1398645225480897,
    0.11981419159397333,
    0.10557980057214614,
    -0.023275300634317965,
    0.1594091170984717,
    -0.25591569617440285,
    0.14406734292143564,
    -0.029165241243977125,
)


def mm(left, right, dims=NN):
    return lax.dot_general(left, right, dims, preferred_element_type=F32)


def params():
    return pltpu.CompilerParams(vmem_limit_bytes=VMEM_LIMIT)


def cost(flops, moved, exps=0):
    return pl.CostEstimate(flops=int(flops), bytes_accessed=int(moved), transcendentals=int(exps))


def gelu_parts(value):
    size = jnp.abs(value)
    t = 1.0 / (1.0 + TAIL_STEP * size)
    poly = jnp.full_like(t, TAIL[-1])
    for term in TAIL[-2::-1]:
        poly = poly * t + term
    bell = jnp.exp(-0.5 * value * value)
    tail = poly * t * bell
    cumulative = jnp.where(value >= 0.0, 1.0 - tail, tail)
    return cumulative, value * (bell * 0.3989422804014327)


def collect(items_s, pieces, table_ref, base, shards):
    block = pieces[0].shape[1]
    for i in range(shards):
        for at, piece in enumerate(pieces):

            @pl.when(table_ref[base + 2 * i] == at)
            def _():
                items_s[i * block : (i + 1) * block, :] = piece[table_ref[base + 2 * i + 1]]


def project_kernel(shards, count, table_ref, w_ref, *refs):
    pieces, out_ref, items_s = refs[:count], refs[count], refs[count + 1]
    step = pl.program_id(0)
    width = items_s.shape[1]
    collect(items_s, pieces, table_ref, step * 2 * shards, shards)
    bias = jnp.sum(w_ref[0, width : width + 3, :].astype(F32), 0, keepdims=True)
    out_ref[0] = (mm(items_s[...], w_ref[0, :width, :]) + bias).astype(BF16)


def whole(shape):
    return pl.BlockSpec(shape, lambda *_: (0,) * len(shape))


def project(pieces, weight, table, length, slots):
    shards, depth, cols = weight.shape
    width = pieces[0].shape[2]
    at = 2 * shards * slots + slots
    return pl.pallas_call(
        functools.partial(project_kernel, shards, len(pieces)),
        grid_spec=pltpu.PrefetchScalarGridSpec(
            num_scalar_prefetch=1,
            grid=(slots,),
            in_specs=[pl.BlockSpec((1, depth, cols), lambda j, t: (t[at + j], 0, 0))]
            + [whole(piece.shape) for piece in pieces],
            out_specs=pl.BlockSpec((1, length, cols), lambda j, t: (j, 0, 0)),
            scratch_shapes=[pltpu.VMEM((length, width), BF16)],
        ),
        out_shape=jax.ShapeDtypeStruct((slots, length, cols), BF16),
        compiler_params=params(),
        cost_estimate=cost(2 * slots * length * width * cols, len(pieces) * pieces[0].size * 2 + slots * length * cols * 2),
    )(table, weight, *pieces)


def weight_back_kernel(shards, count, table_ref, g_ref, *refs):
    pieces, out_ref, items_s = refs[:count], refs[count], refs[count + 1]
    collect(items_s, pieces, table_ref, pl.program_id(0) * 2 * shards, shards)
    out_ref[0] = mm(g_ref[0], items_s[...], TN).astype(BF16)


def weight_back(pieces, grad, table):
    slots, length, cols = grad.shape
    width = pieces[0].shape[2]
    shards = length // pieces[0].shape[1]
    return pl.pallas_call(
        functools.partial(weight_back_kernel, shards, len(pieces)),
        grid_spec=pltpu.PrefetchScalarGridSpec(
            num_scalar_prefetch=1,
            grid=(slots,),
            in_specs=[pl.BlockSpec((1, length, cols), lambda j, t: (j, 0, 0))]
            + [whole(piece.shape) for piece in pieces],
            out_specs=pl.BlockSpec((1, cols, width), lambda j, t: (j, 0, 0)),
            scratch_shapes=[pltpu.VMEM((length, width), BF16)],
        ),
        out_shape=jax.ShapeDtypeStruct((slots, cols, width), BF16),
        compiler_params=params(),
        cost_estimate=cost(2 * slots * length * width * cols, len(pieces) * pieces[0].size * 2 + slots * cols * width * 2),
    )(table, grad, *pieces)


def rows_back_kernel(shards, slots, count, table_ref, w_ref, g_ref, *refs):
    outs, sum_s = refs[:count], refs[count]
    block, width = outs[0].shape[1:]
    step = pl.program_id(0)
    tail = 2 * shards * slots + step
    first = jnp.logical_or(step == 0, table_ref[tail] != table_ref[jnp.maximum(tail - 1, 0)])
    last = jnp.logical_or(
        step == slots - 1, table_ref[tail] != table_ref[jnp.minimum(tail + 1, 2 * shards * slots + slots - 1)]
    )

    @pl.when(step == 0)
    def _():
        for out in outs:
            out[...] = jnp.zeros_like(out)

    part = mm(g_ref[0], w_ref[0, :width, :], NT)

    @pl.when(first)
    def _():
        sum_s[...] = part

    @pl.when(jnp.logical_not(first))
    def _():
        sum_s[...] += part

    @pl.when(last)
    def _():
        for i in range(shards):
            base = step * 2 * shards + 2 * i
            for at, out in enumerate(outs):

                @pl.when(table_ref[base] == at)
                def _():
                    out[table_ref[base + 1]] = sum_s[i * block : (i + 1) * block, :].astype(BF16)


def rows_back(grad, weight, table, block, count, blocks, width):
    shards, depth, cols = weight.shape
    slots, length = grad.shape[:2]
    at = 2 * shards * slots + slots
    piece = (blocks, block, width)
    return pl.pallas_call(
        functools.partial(rows_back_kernel, shards, slots, count),
        grid_spec=pltpu.PrefetchScalarGridSpec(
            num_scalar_prefetch=1,
            grid=(slots,),
            in_specs=[
                pl.BlockSpec((1, depth, cols), lambda j, t: (t[at + j], 0, 0)),
                pl.BlockSpec((1, length, cols), lambda j, t: (j, 0, 0)),
            ],
            out_specs=[whole(piece)] * count,
            scratch_shapes=[pltpu.VMEM((length, width), F32)],
        ),
        out_shape=[jax.ShapeDtypeStruct(piece, BF16)] * count,
        compiler_params=params(),
        cost_estimate=cost(2 * slots * length * width * cols, count * blocks * block * width * 2 + grad.size * 2),
    )(table, weight, grad)


def attend_kernel(heads, block, place_ref, x_ref, ctx_ref, lse_ref, keys_s, values_s):
    step = pl.program_id(1)
    length = x_ref.shape[1]

    @pl.when(step == 0)
    def _():
        for h in range(heads):
            c = h * 3 * HEAD_DIM
            keys_s[h] = x_ref[0, :, c + HEAD_DIM : c + 2 * HEAD_DIM].T
            values_s[h, :, :HEAD_DIM] = x_ref[0, :, c + 2 * HEAD_DIM : c + 3 * HEAD_DIM]
            values_s[h, :, HEAD_DIM:] = jnp.ones((length, HEAD_DIM), BF16)

    rows = pl.ds(pl.multiple_of(step * block, block), block)
    here = x_ref[0, rows, :]
    scores = []
    for h in range(heads):
        c = h * 3 * HEAD_DIM
        query = here[:, c : c + HEAD_DIM] * jnp.asarray(HEAD_DIM**-0.5, BF16)
        scores.append(mm(query, keys_s[h]))
    for h in range(heads):
        row_max = jnp.max(scores[h], 1, keepdims=True)
        probs = jnp.exp(scores[h] - row_max).astype(BF16)
        summed = mm(probs, values_s[h])
        total = summed[:, HEAD_DIM : HEAD_DIM + 1]
        ctx_ref[0, :, h * HEAD_DIM : (h + 1) * HEAD_DIM] = (summed[:, :HEAD_DIM] / total).astype(BF16)
        total_log = row_max + jnp.log(total)
        lse_ref[0, h : h + 1, :] = jnp.broadcast_to(total_log, (block, 128)).T[:1]


def attend(packed, heads, block, places, count):
    units, length, cols = packed.shape
    wide = heads * HEAD_DIM
    steps = length // block
    return pl.pallas_call(
        functools.partial(attend_kernel, heads, block),
        grid_spec=pltpu.PrefetchScalarGridSpec(
            num_scalar_prefetch=1,
            grid=(units, steps),
            in_specs=[pl.BlockSpec((1, length, cols), lambda u, i, t: (u, 0, 0))],
            out_specs=[
                pl.BlockSpec((1, block, wide), lambda u, i, t: (t[u * steps + i], 0, 0)),
                pl.BlockSpec((1, heads, block), lambda u, i, t: (u, 0, i)),
            ],
            scratch_shapes=[
                pltpu.VMEM((heads, HEAD_DIM, length), BF16),
                pltpu.VMEM((heads, length, 2 * HEAD_DIM), BF16),
            ],
        ),
        out_shape=[
            jax.ShapeDtypeStruct((count, block, wide), BF16),
            jax.ShapeDtypeStruct((units, heads, length), F32),
        ],
        compiler_params=params(),
        cost_estimate=cost(units * heads * 16 * length * length * HEAD_DIM, packed.size * 3, units * heads * length * length),
    )(places, packed)


def attend_back_kernel(
    heads, block, place_ref, x_ref, ctx_ref, dctx_ref, lse_ref, grad_ref, sums_ref, keys_t, keys_s, values_s, dk_s, dv_s
):
    step = pl.program_id(1)

    @pl.when(step == 0)
    def _():
        for h in range(heads):
            c = h * 3 * HEAD_DIM
            key = x_ref[0, :, c + HEAD_DIM : c + 2 * HEAD_DIM]
            keys_s[h] = key
            keys_t[h] = key.T
            values_s[h] = x_ref[0, :, c + 2 * HEAD_DIM : c + 3 * HEAD_DIM]
        dk_s[...] = jnp.zeros_like(dk_s)
        dv_s[...] = jnp.zeros_like(dv_s)

    rows = pl.ds(pl.multiple_of(step * block, block), block)
    here = x_ref[0, rows, :]
    grads = dctx_ref[0]
    prods = ctx_ref[0].astype(F32) * grads.astype(F32)
    for h in range(heads):
        c = h * 3 * HEAD_DIM
        part = slice(h * HEAD_DIM, (h + 1) * HEAD_DIM)
        query = here[:, c : c + HEAD_DIM] * jnp.asarray(HEAD_DIM**-0.5, BF16)
        grad = grads[:, part]
        centre = jnp.sum(prods[:, part].T, 0, keepdims=True)
        scores_t = mm(keys_s[h], query.T)
        probs_t = jnp.exp(scores_t - lse_ref[0, h : h + 1, :])
        grad_probs_t = mm(values_s[h], grad.T)
        grad_scores_t = (probs_t * (grad_probs_t - centre)).astype(BF16)
        dv_s[h] += mm(probs_t.astype(BF16), grad)
        dk_s[h] += mm(grad_scores_t, query)
        grad_query_t = mm(keys_t[h], grad_scores_t)
        grad_ref[0, rows, c : c + HEAD_DIM] = (grad_query_t.T * HEAD_DIM**-0.5).astype(BF16)

    @pl.when(step == pl.num_programs(1) - 1)
    def _():
        for h in range(heads):
            c = h * 3 * HEAD_DIM
            grad_ref[0, :, c + HEAD_DIM : c + 2 * HEAD_DIM] = dk_s[h].astype(BF16)
            grad_ref[0, :, c + 2 * HEAD_DIM : c + 3 * HEAD_DIM] = dv_s[h].astype(BF16)
        sums_ref[0] = jnp.sum(grad_ref[0].astype(F32), 0, keepdims=True)


def attend_back(packed, context, grad_context, lse, heads, block, places):
    units, length, cols = packed.shape
    wide = heads * HEAD_DIM
    steps = length // block
    return pl.pallas_call(
        functools.partial(attend_back_kernel, heads, block),
        grid_spec=pltpu.PrefetchScalarGridSpec(
            num_scalar_prefetch=1,
            grid=(units, steps),
            in_specs=[
                pl.BlockSpec((1, length, cols), lambda u, i, t: (u, 0, 0)),
                pl.BlockSpec((1, block, wide), lambda u, i, t: (t[u * steps + i], 0, 0)),
                pl.BlockSpec((1, block, wide), lambda u, i, t: (t[u * steps + i], 0, 0)),
                pl.BlockSpec((1, heads, block), lambda u, i, t: (u, 0, i)),
            ],
            out_specs=[
                pl.BlockSpec((1, length, cols), lambda u, i, t: (u, 0, 0)),
                pl.BlockSpec((1, 1, cols), lambda u, i, t: (u, 0, 0)),
            ],
            scratch_shapes=[
                pltpu.VMEM((heads, HEAD_DIM, length), BF16),
                pltpu.VMEM((heads, length, HEAD_DIM), BF16),
                pltpu.VMEM((heads, length, HEAD_DIM), BF16),
                pltpu.VMEM((heads, length, HEAD_DIM), F32),
                pltpu.VMEM((heads, length, HEAD_DIM), F32),
            ],
        ),
        out_shape=[
            jax.ShapeDtypeStruct((units, length, cols), BF16),
            jax.ShapeDtypeStruct((units, 1, cols), F32),
        ],
        compiler_params=params(),
        cost_estimate=cost(units * heads * 40 * length * length * HEAD_DIM, packed.size * 5, units * heads * length * length),
    )(places, packed, context, grad_context, lse)


def feed_kernel(
    parts, x_ref, g_ref, widen_ref, narrow_ref, bias_ref, out_ref, dx_ref, hidden_ref, pre_ref, bias_grad_ref, out_s, dx_s
):
    step = pl.program_id(0)
    some, count, depth, tile = widen_ref.shape
    piece = depth // parts
    widen = jnp.concatenate([widen_ref[a].reshape(count * depth, tile) for a in range(some)], 1)
    narrow = jnp.concatenate(
        [
            jnp.concatenate(
                [narrow_ref[a, :, c * piece : (c + 1) * piece, :].reshape(tile, tile) for c in range(parts)], 1
            )
            for a in range(some)
        ],
        0,
    )
    bias = jnp.concatenate(
        [jnp.sum(bias_ref[a, 0, 0:3, :].astype(F32), 0, keepdims=True) for a in range(some)], 1
    )
    pre = mm(x_ref[...], widen) + bias
    cumulative, slope = gelu_parts(pre)
    hidden = (pre * cumulative).astype(BF16)
    grad_pre = (mm(g_ref[...], narrow, NT) * (cumulative + slope)).astype(BF16)
    hidden_ref[0] = hidden
    pre_ref[0] = grad_pre
    bias_grad_ref[0] = jnp.sum(grad_pre.astype(F32), 0, keepdims=True)
    out = mm(hidden, narrow)
    dx = mm(grad_pre, widen, NT)

    @pl.when(step == 0)
    def _():
        out_s[...] = out
        dx_s[...] = dx

    @pl.when(step > 0)
    def _():
        out_s[...] += out
        dx_s[...] += dx

    @pl.when(step == pl.num_programs(0) - 1)
    def _():
        out_ref[...] = out_s[...].astype(out_ref.dtype)
        dx_ref[...] = dx_s[...].astype(dx_ref.dtype)


def feed(normed, grad, rest, bias_at, some, dtype):
    shards, count, _, tile = rest.shape
    rows, width = normed.shape
    depth = width // count
    parts = width // tile
    steps = shards // some
    unit_spec = pl.BlockSpec((1, rows, some * tile), lambda m: (m, 0, 0))
    return pl.pallas_call(
        functools.partial(feed_kernel, parts),
        grid=(steps,),
        in_specs=[
            whole((rows, width)),
            whole((rows, width)),
            pl.BlockSpec((some, count, depth, tile), lambda m: (m, 0, 0, 0)),
            pl.BlockSpec((some, count, depth, tile), lambda m: (m, 0, 1, 0)),
            pl.BlockSpec((some, 1, 16, tile), lambda m: (m, 0, bias_at // 16, 0)),
        ],
        out_specs=[
            whole((rows, width)),
            whole((rows, width)),
            unit_spec,
            unit_spec,
            pl.BlockSpec((1, 1, some * tile), lambda m: (m, 0, 0)),
        ],
        out_shape=[
            jax.ShapeDtypeStruct((rows, width), dtype),
            jax.ShapeDtypeStruct((rows, width), dtype),
            jax.ShapeDtypeStruct((steps, rows, some * tile), BF16),
            jax.ShapeDtypeStruct((steps, rows, some * tile), BF16),
            jax.ShapeDtypeStruct((steps, 1, some * tile), F32),
        ],
        scratch_shapes=[pltpu.VMEM((rows, width), F32), pltpu.VMEM((rows, width), F32)],
        compiler_params=params(),
        cost_estimate=cost(8 * shards * rows * width * tile, rest.size * 2 + rows * width * 28, rows * shards * tile),
    )(normed, grad, rest, rest, rest)


def feed_grads_kernel(*refs):
    out_ref = refs[-1]
    some, count, both, width = out_ref.shape
    piece = both // 2
    widen = narrow = 0.0
    for at in range(0, len(refs) - 1, 4):
        x_ref, g_ref, hidden_ref, pre_ref = refs[at : at + 4]
        widen += mm(pre_ref[0], x_ref[...], TN)
        narrow += mm(hidden_ref[0], g_ref[...], TN)
    out_ref[:, :, :piece, :] = widen.astype(BF16).reshape(some, count, piece, width)
    out_ref[:, :, piece:, :] = narrow.astype(BF16).reshape(some, count, piece, width)


def feed_grads(feed_parts, count, some, extra):
    steps, _, tiles = feed_parts[0][2].shape
    width = feed_parts[0][0].shape[1]
    both = 2 * tiles // some // count
    specs, rows_all = [], 0
    for part in feed_parts:
        rows = part[0].shape[0]
        rows_all += rows
        unit_spec = pl.BlockSpec((1, rows, tiles), lambda m: (m, 0, 0))
        specs += [whole((rows, width)), whole((rows, width)), unit_spec, unit_spec]
    return pl.pallas_call(
        feed_grads_kernel,
        grid=(steps,),
        in_specs=specs,
        out_specs=pl.BlockSpec((some, count, both, width), lambda m: (m, 0, 0, 0)),
        out_shape=jax.ShapeDtypeStruct((steps * some, count, both + extra, width), BF16),
        compiler_params=params(),
        cost_estimate=cost(4 * steps * rows_all * width * tiles, steps * rows_all * tiles * 4 + steps * tiles * width * 4),
    )(*[array for part in feed_parts for array in part])


def merge_kernel(shards, slots, place_ref, got_ref, w_ref, start_ref, vec_ref, ctx_ref, middle_ref, normed_ref):
    b = pl.program_id(0)
    wide = got_ref.shape[-1]
    for p in range(shards):
        ctx_ref[:, p * wide : (p + 1) * wide] = got_ref[place_ref[b * shards + p]]
    middle = start_ref[...] + mm(ctx_ref[...], w_ref[...]) + vec_ref[0:1, :]
    middle_ref[...] = middle
    normal, _ = norm_parts(middle)
    normed_ref[...] = (normal * vec_ref[1:2, :] + vec_ref[2:3, :]).astype(BF16)


def merge(got, weight, start, vectors, places, slots):
    count, block, wide = got.shape
    rows, width = start.shape
    shards = width // wide
    row_spec = pl.BlockSpec((block, width), lambda b, t: (b, 0))
    return pl.pallas_call(
        functools.partial(merge_kernel, shards, slots),
        grid_spec=pltpu.PrefetchScalarGridSpec(
            num_scalar_prefetch=1,
            grid=(slots,),
            in_specs=[
                pl.BlockSpec(got.shape, lambda b, t: (0, 0, 0)),
                pl.BlockSpec(weight.shape, lambda b, t: (0, 0)),
                row_spec,
                pl.BlockSpec(vectors.shape, lambda b, t: (0, 0)),
            ],
            out_specs=[row_spec, row_spec, row_spec],
        ),
        out_shape=[
            jax.ShapeDtypeStruct((rows, width), BF16),
            jax.ShapeDtypeStruct((rows, width), F32),
            jax.ShapeDtypeStruct((rows, width), BF16),
        ],
        compiler_params=params(),
        cost_estimate=cost(2 * rows * width * width, rows * width * 20),
    )(places, got, weight, start, vectors)


def merge_back_kernel(shards, count, shard_ref, g_ref, w_ref, out_ref, dctx_s):
    wide = out_ref.shape[-1]
    grad = g_ref[...]
    for p in range(shards):
        dctx_s[p] = mm(grad, w_ref[p * wide : (p + 1) * wide, :], NT).astype(BF16)
    for i in range(count):
        out_ref[i] = dctx_s[shard_ref[i]]


def merge_back(grad, weight, shard_of, wide):
    rows, width = grad.shape
    shards = width // wide
    count = shard_of.shape[0]
    return pl.pallas_call(
        functools.partial(merge_back_kernel, shards, count),
        grid_spec=pltpu.PrefetchScalarGridSpec(
            num_scalar_prefetch=1,
            grid=(1,),
            in_specs=[
                pl.BlockSpec((rows, width), lambda b, t: (0, 0)),
                pl.BlockSpec((width, width), lambda b, t: (0, 0)),
            ],
            out_specs=pl.BlockSpec((count, rows, wide), lambda b, t: (0, 0, 0)),
            scratch_shapes=[pltpu.VMEM((shards, rows, wide), BF16)],
        ),
        out_shape=jax.ShapeDtypeStruct((count, rows, wide), BF16),
        compiler_params=params(),
        cost_estimate=cost(2 * rows * width * width, rows * width * 8),
    )(shard_of, grad, weight)


def norm_parts(value):
    mean = jnp.mean(value, -1, keepdims=True)
    centred = value - mean
    scale = lax.rsqrt(jnp.mean(centred * centred, -1, keepdims=True) + EPSILON)
    return centred * scale, scale


def norm_back(normal, scale, gain, grad):
    grad_x = grad * gain
    mean = jnp.mean(grad_x, -1, keepdims=True)
    along = jnp.mean(grad_x * normal, -1, keepdims=True)
    return (
        (grad_x - mean - normal * along) * scale,
        jnp.sum(grad * normal, 0),
        jnp.sum(grad, 0),
    )


def share_of(array, at, count):
    share = array.shape[0] // count
    return lax.dynamic_slice_in_dim(array, at * share, share, 0)


def on_device(
    tokens,
    cotangent,
    group_items,
    dataset_ids,
    lead_hours,
    set_weights,
    lead_weight,
    lead_shift,
    norm_one_gain,
    norm_one_shift,
    heads_weight,
    heads_bias,
    merge_weight,
    merge_bias,
    norm_two_gain,
    norm_two_shift,
    widen_weight,
    widen_bias,
    narrow_weight,
    narrow_bias,
):
    shards = lax.axis_size("mp")
    copies = lax.axis_size("dp")
    rows_here, width = tokens.shape
    group_rows = rows_here * shards
    slots = dataset_ids.shape[0]
    length = group_rows // slots
    block = rows_here // slots
    cols = heads_weight.shape[1]
    heads_here = cols // (3 * HEAD_DIM)
    wide = heads_here * HEAD_DIM
    tile = widen_weight.shape[1] // 2
    parts = width // tile
    count = copies // 2
    some = 4
    dp_at = lax.axis_index("dp")
    mp_at = lax.axis_index("mp")
    both = ("dp", "mp")

    def attention_device(group, k):
        return (group // 2 * 2 + k % 2) * shards + k // 2 * 2 + group % 2

    def row_device(group, k):
        return group * shards + k

    groups = range(copies)
    spots = range(shards)

    def meet(k_rows, k_unit):
        return any(
            (slots * k_rows + b) // shards == (slots * k_unit + j) // shards
            for b in range(slots)
            for j in range(slots)
        )

    core_swap = [(g, g + 1 - g % 2 * 2) for g in groups]
    half_swap = [(g, g ^ 2) for g in groups]
    half_at = dp_at // 2 % 2
    piece_at = dp_at // 4 * 2 + dp_at % 2
    plane = [[k * copies + g for k in spots for g in groups if g // 2 % 2 == h] for h in range(2)]
    row_swap = [(k, k + 1 - k % 2 * 2) for k in spots]
    reach = max(abs(a // 2 - b // 2) for a in spots for b in spots if meet(a, b))
    classes = []
    for s in sorted(range(1 - shards, shards), key=abs):
        pairs = [(k, k + s) for k in spots if 0 <= k + s < shards and meet(k + s, k)]
        for known in classes:
            if not any(a == c or b == d for a, b in pairs for c, d in known):
                known += pairs
                break
        else:
            if pairs:
                classes.append(pairs)
    color = [[0] * shards for _ in spots]
    senders = [[0] * shards for _ in classes]
    for i, pairs in enumerate(classes):
        for unit, rows in pairs:
            color[unit][rows] = i
            senders[i][rows] = unit
    color = jnp.asarray(color, jnp.int32)
    senders = jnp.asarray(senders, jnp.int32)

    def extents(pairs):
        ranges = []
        for unit, rows in pairs:
            shared = [
                (j, b)
                for j in range(slots)
                for b in range(slots)
                if (slots * rows + b) // shards == (slots * unit + j) // shards
            ]
            ranges.append([(min(part), max(part) + 1) for part in zip(*shared)])
        sizes = [max(r[at][1] - r[at][0] for r in ranges) for at in range(2)]
        unit_starts = [[0] * shards for _ in range(2)]
        row_starts = [[0] * shards for _ in range(2)]
        for (unit, rows), r in zip(pairs, ranges):
            for at in range(2):
                unit_starts[at][unit] = row_starts[at][rows] = min(r[at][0], slots - sizes[at])
        return sizes, unit_starts, row_starts

    def exchange(array, to_rows):
        got = []
        for i, pairs in enumerate(classes):
            sizes, unit_starts, row_starts = extents(pairs)
            ends = [(attention_device(g, unit), row_device(g, rows)) for g in groups for unit, rows in pairs]
            ends = ends if to_rows else back(ends)
            message = array[i]
            if sizes == [slots, slots]:
                got.append(lax.ppermute(message, both, ends))
                continue
            at_unit = [jnp.asarray(part, jnp.int32)[k_here] for part in unit_starts]
            at_rows = [jnp.asarray(part, jnp.int32)[mp_at] for part in row_starts]
            at_from, at_to = (at_unit, at_rows) if to_rows else (at_rows, at_unit)
            some_part = lax.dynamic_slice(message, (*at_from, 0, 0), (*sizes, *message.shape[2:]))
            some_part = lax.ppermute(some_part, both, ends)
            got.append((some_part, at_to))
        return got

    def together(got, shape):
        whole_ones = [
            lax.dynamic_update_slice(jnp.zeros(shape, BF16), part[0], (*part[1], 0, 0))
            if isinstance(part, tuple)
            else part
            for part in got
        ]
        return jnp.stack(whole_ones).reshape(-1, *shape[2:])

    def far(step):
        return [
            (attention_device(g, k), row_device(g, k + 2 * step))
            for g in groups
            for k in spots
            if 0 <= k + 2 * step < shards and any(meet(k + 2 * step, k // 2 * 2 + b) for b in range(2))
        ]

    def back(pairs):
        return [(b, a) for a, b in pairs]

    steps = range(-reach, reach + 1)

    k_here = mp_at // 2 * 2 + dp_at % 2
    unit_ids = slots * k_here + jnp.arange(slots, dtype=jnp.int32)
    unit_items = unit_ids // shards
    unit_blocks = unit_items[:, None] * shards + jnp.arange(shards, dtype=jnp.int32)[None, :]
    block_spots = unit_blocks // slots
    table = jnp.stack(
        [
            (block_spots + dp_at) % 2,
            (block_spots // 2 - mp_at // 2 + reach) * slots + unit_blocks % slots,
        ],
        2,
    )
    table = jnp.concatenate([table.reshape(-1), unit_items, unit_ids % shards]).astype(jnp.int32)
    counting = jnp.arange(slots, dtype=jnp.int32)
    unit_places = (
        (color[k_here, block_spots] * slots + counting[:, None]) * slots + unit_blocks % slots
    ).reshape(-1)
    row_units = ((slots * mp_at + counting) // shards * shards)[:, None] + jnp.arange(
        shards, dtype=jnp.int32
    )[None, :]
    row_places = (
        (color[row_units // slots, mp_at] * slots + row_units % slots) * slots + counting[:, None]
    ).reshape(-1)
    wanted = ((slots * senders[:, mp_at][:, None] + counting[None, :]) % shards).reshape(-1)

    def weight_pairs(j):
        return [
            (g * shards + (slots * k + j) % shards, attention_device(g, k)) for g in groups for k in spots
        ]

    def exact_rows(vector, pad):
        high = vector.astype(BF16)
        left = vector - high.astype(F32)
        middle = left.astype(BF16)
        low = (left - middle.astype(F32)).astype(BF16)
        return jnp.pad(jnp.stack([high, middle, low]), ((0, pad - 3), (0, 0)))

    bias_heads = heads_bias.reshape(heads_here, 2, HEAD_DIM)
    full_bias = jnp.stack(
        [bias_heads[:, 0], jnp.zeros_like(bias_heads[:, 0]), bias_heads[:, 1]], 1
    ).reshape(-1)
    heads_rows = jnp.concatenate([heads_weight, exact_rows(full_bias, 16 * count)], 0)
    heads_piece = share_of(heads_rows, piece_at, count)
    heads_piece, tokens = lax.optimization_barrier((heads_piece, tokens))
    heads_all = lax.all_gather(heads_piece, BOTH, axis=0, tiled=True, axis_index_groups=plane)
    heads_all = heads_all.reshape(shards, -1, cols)

    row_ids = mp_at * rows_here + jnp.arange(rows_here, dtype=jnp.int32)
    slot_ids = jnp.arange(slots, dtype=jnp.int32)
    slot_table = ((row_ids // length)[:, None] == slot_ids[None, :]).astype(F32)
    lead_scaled = jnp.sum(slot_table * (lead_hours.astype(F32) / 100.0)[None, :], 1)
    live = (slot_ids < group_items[0]).astype(F32)
    set_ids = jnp.arange(set_weights.shape[0], dtype=jnp.int32)
    set_match = (dataset_ids[:, None] == set_ids[None, :]).astype(F32)
    item_weight = live * jnp.sum(set_match * set_weights[None, :], 1)
    row_weight = jnp.sum(slot_table * item_weight[None, :], 1)

    start_state = tokens + lead_scaled[:, None] * lead_weight + lead_shift
    first_normal, first_scale = norm_parts(start_state)
    normed_one = (first_normal * norm_one_gain + norm_one_shift).astype(BF16)

    def fold(part):
        return jnp.concatenate(jnp.split(part, parts, 1), 0)

    rest = jnp.concatenate(
        [
            share_of(lax.dynamic_slice_in_dim(widen_weight, half_at * tile, tile, 1), piece_at, count),
            fold(share_of(share_of(narrow_weight, half_at, 2), piece_at, count)),
            fold(share_of(merge_weight, piece_at, count)),
            exact_rows(share_of(widen_bias, half_at, 2), 16),
        ],
        0,
    )
    merge_rows = merge_weight.shape[0] // count
    merge_at = 2 * (width // count)
    bias_at = merge_at + merge_rows * parts

    own = jnp.stack([lax.ppermute(normed_one, both, back(far(o))) for o in steps])
    grad_out = cotangent * row_weight[:, None]
    grad_low = grad_out.astype(BF16)
    own, rest, grad_low, live_items = lax.optimization_barrier((own, rest, grad_low, group_items))
    item_total = lax.psum(live_items.astype(F32)[0], "dp")
    rest = lax.all_gather(rest, BOTH, axis=0, tiled=True, axis_index_groups=plane)
    rest = rest.reshape(shards, count, -1, tile)
    their_grad = lax.ppermute(grad_low, "dp", half_swap)
    other = lax.ppermute(own, "dp", core_swap)
    other, item_total = lax.optimization_barrier((other, item_total))
    pieces = [part.reshape(-1, block, width) for part in (own, other)]

    packed = project(pieces, heads_all, table, length, slots)
    messages = len(classes) * slots * slots
    message = (slots, slots, block, wide)
    context, lse = attend(packed, heads_here, block, unit_places, messages)
    context_got = together(exchange(context.reshape(-1, *message), True), message)
    merge_all = rest[:, :, merge_at:bias_at, :].reshape(shards, count, parts, merge_rows, tile)
    merge_all = merge_all.transpose(0, 1, 3, 2, 4).reshape(width, width)
    merge_vectors = jnp.pad(jnp.stack([merge_bias, norm_two_gain, norm_two_shift]), ((0, 5), (0, 0)))
    context_rows, middle, normed_two = merge(
        context_got, merge_all, start_state, merge_vectors, row_places, slots
    )
    second_normal, second_scale = norm_parts(middle)

    narrow_bias_grad = jnp.sum(grad_low.astype(F32), 0)
    chunk = rows_here // 2
    chunks = [slice(0, chunk), slice(chunk, rows_here)]
    their_normed = [lax.ppermute(normed_two[rows], "dp", half_swap) for rows in chunks]
    fed, grad_norm_two, hidden, grad_pre, widen_bias_grad = feed(
        normed_two, grad_low, rest, bias_at, some, F32
    )
    feed_parts = [(normed_two, grad_low, hidden, grad_pre)]
    their_fed, their_dx = [], []
    for i, rows in enumerate(chunks):
        their_normed[i], fed = lax.optimization_barrier((their_normed[i], fed))
        their = (their_normed[i], their_grad[rows])
        part_fed, part_dx, hidden, grad_pre, part_bias = feed(*their, rest, bias_at, some, BF16)
        feed_parts.append(their + (hidden, grad_pre))
        widen_bias_grad += part_bias
        their_fed.append(part_fed)
        their_dx.append(lax.ppermute(part_dx, "dp", half_swap))
        fed = lax.optimization_barrier((fed, part_dx))[0]
    grads_one = feed_grads(feed_parts, count, some, merge_weight.shape[0] // copies)
    their_dx[-1], grads_one, *their_fed = lax.optimization_barrier((their_dx[-1], grads_one, *their_fed))
    grad_norm_two = grad_norm_two + jnp.concatenate(their_dx).astype(F32)
    their_fed = lax.ppermute(jnp.concatenate(their_fed), "dp", half_swap)
    widen_bias_grad = widen_bias_grad.reshape(shards, 1, tile)
    widen_bias_grad = jnp.where(
        jnp.arange(2, dtype=jnp.int32)[None, :, None] == half_at, widen_bias_grad, 0.0
    )
    grad_mid_norm, norm_two_gain_grad, norm_two_shift_grad = norm_back(
        second_normal, second_scale, norm_two_gain, grad_norm_two
    )
    grad_middle = grad_out + grad_mid_norm
    grad_mid_low = grad_middle.astype(BF16)
    merge_bias_grad = jnp.sum(grad_mid_low.astype(F32), 0)
    grad_context = merge_back(grad_mid_low, merge_all, wanted, wide)
    grad_context = exchange(grad_context.reshape(-1, *message), False)
    grad_context = together(grad_context, message)
    merge_weight_grad = mm(context_rows, grad_mid_low, TN).astype(BF16)
    merge_weight_grad = merge_weight_grad.reshape(shards, copies // 4, 2, 2, -1, width)
    kept = lax.dynamic_index_in_dim(merge_weight_grad, half_at, 2, False)
    sent = lax.dynamic_index_in_dim(merge_weight_grad, 1 - half_at, 2, False)
    kept = kept.astype(F32) + lax.ppermute(sent, "dp", half_swap).astype(F32)
    grads_one = grads_one.at[:, :, 2 * (tile // count) :].set(
        kept.astype(BF16).reshape(shards, count, -1, width)
    )
    grads_one = lax.psum_scatter(
        grads_one.reshape(-1, width), BOTH, scatter_dimension=0, tiled=True, axis_index_groups=plane
    )
    grad_packed, unit_sums = attend_back(
        packed, context, grad_context, lse, heads_here, block, unit_places
    )
    grad_packed, their_fed = lax.optimization_barrier((grad_packed, their_fed))
    activations = middle + fed + their_fed.astype(F32) + narrow_bias
    unit_grads = weight_back(pieces, grad_packed, table)
    heads_parts = [lax.ppermute(unit_grads[j], both, back(weight_pairs(j))) for j in range(slots)]
    grad_packed, unit_grads = lax.optimization_barrier((grad_packed, unit_grads))
    own_dx, other_dx = rows_back(grad_packed, heads_all, table, block, 2, len(steps) * slots, width)

    other_dx = lax.ppermute(other_dx, "dp", core_swap)
    other_dx, *heads_parts = lax.optimization_barrier((other_dx, *heads_parts))
    other_dx = other_dx.reshape(-1, rows_here, width)
    own_dx = own_dx.reshape(-1, rows_here, width)
    pair_dx = [(own_dx[i].astype(F32) + other_dx[i].astype(F32)).astype(BF16) for i in range(len(steps))]
    grad_norm_one = [lax.ppermute(pair_dx[i], both, far(o)) for i, o in enumerate(steps)]

    heads_total = sum(part.astype(F32) for part in heads_parts).astype(BF16)
    for bit in range((copies - 1).bit_length()):
        over = lax.ppermute(heads_total, "dp", [(g, g ^ 1 << bit) for g in groups])
        heads_total = (heads_total.astype(F32) + over.astype(F32)).astype(BF16)
    grad_norm_one[-1], heads_total = lax.optimization_barrier((grad_norm_one[-1], heads_total))
    grad_norm_one = sum(part.astype(F32) for part in grad_norm_one)
    heads_bias_grad = jnp.sum(
        jnp.where(
            (unit_ids % shards)[:, None, None] == jnp.arange(shards, dtype=jnp.int32)[None, :, None],
            unit_sums,
            0.0,
        ),
        0,
    )

    grad_start_norm, norm_one_gain_grad, norm_one_shift_grad = norm_back(
        first_normal, first_scale, norm_one_gain, grad_norm_one
    )
    grad_start = grad_middle + grad_start_norm
    lead_weight_grad = jnp.sum(grad_start * lead_scaled[:, None], 0)
    lead_shift_grad = jnp.sum(grad_start, 0)
    vectors = (
        lead_weight_grad,
        lead_shift_grad,
        norm_one_gain_grad,
        norm_one_shift_grad,
        merge_bias_grad,
        norm_two_gain_grad,
        norm_two_shift_grad,
        narrow_bias_grad,
    )
    vectors = jnp.concatenate(
        [jnp.stack(vectors).reshape(-1), widen_bias_grad.reshape(-1), heads_bias_grad.reshape(-1)]
    )
    hops = [
        (axis, [(i, i ^ 1 << bit) for i in range(size)])
        for axis, size in (("dp", copies), ("mp", shards))
        for bit in range((size - 1).bit_length())
    ]
    for axis, pairs in hops:
        vectors += lax.ppermute(vectors, axis, pairs)
    vectors /= item_total
    heads_total = heads_total.astype(F32)
    shared = vectors[: 8 * width].reshape(8, width)
    place = lax.axis_index("mp")
    widen_bias_total = lax.dynamic_slice_in_dim(vectors, 8 * width + place * 2 * tile, 2 * tile, 0)
    heads_bias_total = lax.dynamic_slice_in_dim(
        vectors, 8 * width + shards * 2 * tile + place * cols, cols, 0
    ).reshape(heads_here, 3, HEAD_DIM)
    heads_bias_total = jnp.stack([heads_bias_total[:, 0], heads_bias_total[:, 2]], 1).reshape(-1)

    grads_one = lax.all_gather(grads_one, "dp", axis=0, tiled=True).astype(F32) / item_total
    piece = tile // count
    grads_one = grads_one.reshape(copies // 4, 2, 2, -1, width).transpose(1, 0, 2, 3, 4)
    widen_total = grads_one[:, :, :, :piece].reshape(2 * tile, width).T
    narrow_total = grads_one[:, :, :, piece : 2 * piece].reshape(2 * tile, width)
    merge_total = grads_one[:, :, :, 2 * piece :].transpose(1, 0, 2, 3, 4).reshape(-1, width)
    heads_total = heads_total.T / item_total
    return (
        activations,
        grad_start / item_total,
        shared[0],
        shared[1],
        shared[2],
        shared[3],
        heads_total,
        heads_bias_total,
        merge_total,
        shared[4],
        shared[5],
        shared[6],
        widen_total,
        widen_bias_total,
        narrow_total,
        shared[7],
    )


def solution(mesh):
    return jax.shard_map(
        on_device,
        mesh=mesh,
        in_specs=(
            P(("dp", "mp"), None),
            P(("dp", "mp"), None),
            P("dp"),
            P("dp"),
            P("dp"),
            P(),
            P(),
            P(),
            P(),
            P(),
            P(None, "mp"),
            P("mp"),
            P("mp", None),
            P(),
            P(),
            P(),
            P(None, "mp"),
            P("mp"),
            P("mp", None),
            P(),
        ),
        out_specs=(
            P(("dp", "mp"), None),
            P(("dp", "mp"), None),
            P(),
            P(),
            P(),
            P(),
            P(None, "mp"),
            P("mp"),
            P("mp", None),
            P(),
            P(),
            P(),
            P(None, "mp"),
            P("mp"),
            P("mp", None),
            P(),
        ),
        check_vma=False,
    )
```

```python
import functools

import jax
import jax.numpy as jnp
from jax import lax
from jax.experimental import pallas as pl
from jax.experimental.pallas import tpu as pltpu
from jax.sharding import PartitionSpec as P

HEAD_DIM = 64
EPSILON = 1e-05
F32 = jnp.float32
BF16 = jnp.bfloat16
NN = (((1,), (0,)), ((), ()))
NT = (((1,), (1,)), ((), ()))
TN = (((0,), (0,)), ((), ()))
BOTH = ("mp", "dp")
VMEM_LIMIT = 56 * 2**20

TAIL_STEP = 0.35
TAIL = (
    0.13962124730886327,
    0.1398645225480897,
    0.11981419159397333,
    0.10557980057214614,
    -0.023275300634317965,
    0.1594091170984717,
    -0.25591569617440285,
    0.14406734292143564,
    -0.029165241243977125,
)


def mm(left, right, dims=NN):
    return lax.dot_general(left, right, dims, preferred_element_type=F32)


def params():
    return pltpu.CompilerParams(vmem_limit_bytes=VMEM_LIMIT)


def cost(flops, moved, exps=0):
    return pl.CostEstimate(flops=int(flops), bytes_accessed=int(moved), transcendentals=int(exps))


def gelu_parts(value):
    size = jnp.abs(value)
    t = 1.0 / (1.0 + TAIL_STEP * size)
    poly = jnp.full_like(t, TAIL[-1])
    for term in TAIL[-2::-1]:
        poly = poly * t + term
    bell = jnp.exp(-0.5 * value * value)
    tail = poly * t * bell
    cumulative = jnp.where(value >= 0.0, 1.0 - tail, tail)
    return cumulative, value * (bell * 0.3989422804014327)


def collect(items_s, pieces, table_ref, base, shards):
    block = pieces[0].shape[1]
    for i in range(shards):
        for at, piece in enumerate(pieces):

            @pl.when(table_ref[base + 2 * i] == at)
            def _():
                items_s[i * block : (i + 1) * block, :] = piece[table_ref[base + 2 * i + 1]]


def project_kernel(shards, count, table_ref, w_ref, *refs):
    pieces, out_ref, items_s = refs[:count], refs[count], refs[count + 1]
    step = pl.program_id(0)
    width = items_s.shape[1]
    collect(items_s, pieces, table_ref, step * 2 * shards, shards)
    bias = jnp.sum(w_ref[0, width : width + 3, :].astype(F32), 0, keepdims=True)
    out_ref[0] = (mm(items_s[...], w_ref[0, :width, :]) + bias).astype(BF16)


def whole(shape):
    return pl.BlockSpec(shape, lambda *_: (0,) * len(shape))


def project(pieces, weight, table, length, slots):
    shards, depth, cols = weight.shape
    width = pieces[0].shape[2]
    at = 2 * shards * slots + slots
    return pl.pallas_call(
        functools.partial(project_kernel, shards, len(pieces)),
        grid_spec=pltpu.PrefetchScalarGridSpec(
            num_scalar_prefetch=1,
            grid=(slots,),
            in_specs=[pl.BlockSpec((1, depth, cols), lambda j, t: (t[at + j], 0, 0))]
            + [whole(piece.shape) for piece in pieces],
            out_specs=pl.BlockSpec((1, length, cols), lambda j, t: (j, 0, 0)),
            scratch_shapes=[pltpu.VMEM((length, width), BF16)],
        ),
        out_shape=jax.ShapeDtypeStruct((slots, length, cols), BF16),
        compiler_params=params(),
        cost_estimate=cost(2 * slots * length * width * cols, len(pieces) * pieces[0].size * 2 + slots * length * cols * 2),
    )(table, weight, *pieces)


def weight_back_kernel(shards, count, table_ref, g_ref, *refs):
    pieces, out_ref, items_s = refs[:count], refs[count], refs[count + 1]
    collect(items_s, pieces, table_ref, pl.program_id(0) * 2 * shards, shards)
    out_ref[0] = mm(g_ref[0], items_s[...], TN).astype(BF16)


def weight_back(pieces, grad, table):
    slots, length, cols = grad.shape
    width = pieces[0].shape[2]
    shards = length // pieces[0].shape[1]
    return pl.pallas_call(
        functools.partial(weight_back_kernel, shards, len(pieces)),
        grid_spec=pltpu.PrefetchScalarGridSpec(
            num_scalar_prefetch=1,
            grid=(slots,),
            in_specs=[pl.BlockSpec((1, length, cols), lambda j, t: (j, 0, 0))]
            + [whole(piece.shape) for piece in pieces],
            out_specs=pl.BlockSpec((1, cols, width), lambda j, t: (j, 0, 0)),
            scratch_shapes=[pltpu.VMEM((length, width), BF16)],
        ),
        out_shape=jax.ShapeDtypeStruct((slots, cols, width), BF16),
        compiler_params=params(),
        cost_estimate=cost(2 * slots * length * width * cols, len(pieces) * pieces[0].size * 2 + slots * cols * width * 2),
    )(table, grad, *pieces)


def rows_back_kernel(shards, slots, count, table_ref, w_ref, g_ref, *refs):
    outs, sum_s = refs[:count], refs[count]
    block, width = outs[0].shape[1:]
    step = pl.program_id(0)
    tail = 2 * shards * slots + step
    first = jnp.logical_or(step == 0, table_ref[tail] != table_ref[jnp.maximum(tail - 1, 0)])
    last = jnp.logical_or(
        step == slots - 1, table_ref[tail] != table_ref[jnp.minimum(tail + 1, 2 * shards * slots + slots - 1)]
    )

    @pl.when(step == 0)
    def _():
        for out in outs:
            out[...] = jnp.zeros_like(out)

    part = mm(g_ref[0], w_ref[0, :width, :], NT)

    @pl.when(first)
    def _():
        sum_s[...] = part

    @pl.when(jnp.logical_not(first))
    def _():
        sum_s[...] += part

    @pl.when(last)
    def _():
        for i in range(shards):
            base = step * 2 * shards + 2 * i
            for at, out in enumerate(outs):

                @pl.when(table_ref[base] == at)
                def _():
                    out[table_ref[base + 1]] = sum_s[i * block : (i + 1) * block, :].astype(BF16)


def rows_back(grad, weight, table, block, count, blocks, width):
    shards, depth, cols = weight.shape
    slots, length = grad.shape[:2]
    at = 2 * shards * slots + slots
    piece = (blocks, block, width)
    return pl.pallas_call(
        functools.partial(rows_back_kernel, shards, slots, count),
        grid_spec=pltpu.PrefetchScalarGridSpec(
            num_scalar_prefetch=1,
            grid=(slots,),
            in_specs=[
                pl.BlockSpec((1, depth, cols), lambda j, t: (t[at + j], 0, 0)),
                pl.BlockSpec((1, length, cols), lambda j, t: (j, 0, 0)),
            ],
            out_specs=[whole(piece)] * count,
            scratch_shapes=[pltpu.VMEM((length, width), F32)],
        ),
        out_shape=[jax.ShapeDtypeStruct(piece, BF16)] * count,
        compiler_params=params(),
        cost_estimate=cost(2 * slots * length * width * cols, count * blocks * block * width * 2 + grad.size * 2),
    )(table, weight, grad)


def attend_kernel(heads, block, place_ref, x_ref, ctx_ref, lse_ref, keys_s, values_s):
    step = pl.program_id(1)
    length = x_ref.shape[1]

    @pl.when(step == 0)
    def _():
        for h in range(heads):
            c = h * 3 * HEAD_DIM
            keys_s[h] = x_ref[0, :, c + HEAD_DIM : c + 2 * HEAD_DIM].T
            values_s[h, :, :HEAD_DIM] = x_ref[0, :, c + 2 * HEAD_DIM : c + 3 * HEAD_DIM]
            values_s[h, :, HEAD_DIM:] = jnp.ones((length, HEAD_DIM), BF16)

    rows = pl.ds(pl.multiple_of(step * block, block), block)
    here = x_ref[0, rows, :]
    scores = []
    for h in range(heads):
        c = h * 3 * HEAD_DIM
        query = here[:, c : c + HEAD_DIM] * jnp.asarray(HEAD_DIM**-0.5, BF16)
        scores.append(mm(query, keys_s[h]))
    for h in range(heads):
        row_max = jnp.max(scores[h], 1, keepdims=True)
        probs = jnp.exp(scores[h] - row_max).astype(BF16)
        summed = mm(probs, values_s[h])
        total = summed[:, HEAD_DIM : HEAD_DIM + 1]
        ctx_ref[0, :, h * HEAD_DIM : (h + 1) * HEAD_DIM] = (summed[:, :HEAD_DIM] / total).astype(BF16)
        total_log = row_max + jnp.log(total)
        lse_ref[0, h : h + 1, :] = jnp.broadcast_to(total_log, (block, 128)).T[:1]


def attend(packed, heads, block, places, count):
    units, length, cols = packed.shape
    wide = heads * HEAD_DIM
    steps = length // block
    return pl.pallas_call(
        functools.partial(attend_kernel, heads, block),
        grid_spec=pltpu.PrefetchScalarGridSpec(
            num_scalar_prefetch=1,
            grid=(units, steps),
            in_specs=[pl.BlockSpec((1, length, cols), lambda u, i, t: (u, 0, 0))],
            out_specs=[
                pl.BlockSpec((1, block, wide), lambda u, i, t: (t[u * steps + i], 0, 0)),
                pl.BlockSpec((1, heads, block), lambda u, i, t: (u, 0, i)),
            ],
            scratch_shapes=[
                pltpu.VMEM((heads, HEAD_DIM, length), BF16),
                pltpu.VMEM((heads, length, 2 * HEAD_DIM), BF16),
            ],
        ),
        out_shape=[
            jax.ShapeDtypeStruct((count, block, wide), BF16),
            jax.ShapeDtypeStruct((units, heads, length), F32),
        ],
        compiler_params=params(),
        cost_estimate=cost(units * heads * 16 * length * length * HEAD_DIM, packed.size * 3, units * heads * length * length),
    )(places, packed)


def attend_back_kernel(
    heads, block, place_ref, x_ref, ctx_ref, dctx_ref, lse_ref, grad_ref, sums_ref, keys_t, keys_s, values_s, dk_s, dv_s
):
    step = pl.program_id(1)

    @pl.when(step == 0)
    def _():
        for h in range(heads):
            c = h * 3 * HEAD_DIM
            key = x_ref[0, :, c + HEAD_DIM : c + 2 * HEAD_DIM]
            keys_s[h] = key
            keys_t[h] = key.T
            values_s[h] = x_ref[0, :, c + 2 * HEAD_DIM : c + 3 * HEAD_DIM]
        dk_s[...] = jnp.zeros_like(dk_s)
        dv_s[...] = jnp.zeros_like(dv_s)

    rows = pl.ds(pl.multiple_of(step * block, block), block)
    here = x_ref[0, rows, :]
    grads = dctx_ref[0]
    prods = ctx_ref[0].astype(F32) * grads.astype(F32)
    for h in range(heads):
        c = h * 3 * HEAD_DIM
        part = slice(h * HEAD_DIM, (h + 1) * HEAD_DIM)
        query = here[:, c : c + HEAD_DIM] * jnp.asarray(HEAD_DIM**-0.5, BF16)
        grad = grads[:, part]
        centre = jnp.sum(prods[:, part].T, 0, keepdims=True)
        scores_t = mm(keys_s[h], query.T)
        probs_t = jnp.exp(scores_t - lse_ref[0, h : h + 1, :])
        grad_probs_t = mm(values_s[h], grad.T)
        grad_scores_t = (probs_t * (grad_probs_t - centre)).astype(BF16)
        dv_s[h] += mm(probs_t.astype(BF16), grad)
        dk_s[h] += mm(grad_scores_t, query)
        grad_query_t = mm(keys_t[h], grad_scores_t)
        grad_ref[0, rows, c : c + HEAD_DIM] = (grad_query_t.T * HEAD_DIM**-0.5).astype(BF16)

    @pl.when(step == pl.num_programs(1) - 1)
    def _():
        for h in range(heads):
            c = h * 3 * HEAD_DIM
            grad_ref[0, :, c + HEAD_DIM : c + 2 * HEAD_DIM] = dk_s[h].astype(BF16)
            grad_ref[0, :, c + 2 * HEAD_DIM : c + 3 * HEAD_DIM] = dv_s[h].astype(BF16)
        sums_ref[0] = jnp.sum(grad_ref[0].astype(F32), 0, keepdims=True)


def attend_back(packed, context, grad_context, lse, heads, block, places):
    units, length, cols = packed.shape
    wide = heads * HEAD_DIM
    steps = length // block
    return pl.pallas_call(
        functools.partial(attend_back_kernel, heads, block),
        grid_spec=pltpu.PrefetchScalarGridSpec(
            num_scalar_prefetch=1,
            grid=(units, steps),
            in_specs=[
                pl.BlockSpec((1, length, cols), lambda u, i, t: (u, 0, 0)),
                pl.BlockSpec((1, block, wide), lambda u, i, t: (t[u * steps + i], 0, 0)),
                pl.BlockSpec((1, block, wide), lambda u, i, t: (t[u * steps + i], 0, 0)),
                pl.BlockSpec((1, heads, block), lambda u, i, t: (u, 0, i)),
            ],
            out_specs=[
                pl.BlockSpec((1, length, cols), lambda u, i, t: (u, 0, 0)),
                pl.BlockSpec((1, 1, cols), lambda u, i, t: (u, 0, 0)),
            ],
            scratch_shapes=[
                pltpu.VMEM((heads, HEAD_DIM, length), BF16),
                pltpu.VMEM((heads, length, HEAD_DIM), BF16),
                pltpu.VMEM((heads, length, HEAD_DIM), BF16),
                pltpu.VMEM((heads, length, HEAD_DIM), F32),
                pltpu.VMEM((heads, length, HEAD_DIM), F32),
            ],
        ),
        out_shape=[
            jax.ShapeDtypeStruct((units, length, cols), BF16),
            jax.ShapeDtypeStruct((units, 1, cols), F32),
        ],
        compiler_params=params(),
        cost_estimate=cost(units * heads * 40 * length * length * HEAD_DIM, packed.size * 5, units * heads * length * length),
    )(places, packed, context, grad_context, lse)


def feed_kernel(
    parts, x_ref, g_ref, widen_ref, narrow_ref, bias_ref, out_ref, dx_ref, hidden_ref, pre_ref, bias_grad_ref, out_s, dx_s
):
    step = pl.program_id(0)
    some, count, depth, tile = widen_ref.shape
    piece = depth // parts
    widen = jnp.concatenate([widen_ref[a].reshape(count * depth, tile) for a in range(some)], 1)
    narrow = jnp.concatenate(
        [
            jnp.concatenate(
                [narrow_ref[a, :, c * piece : (c + 1) * piece, :].reshape(tile, tile) for c in range(parts)], 1
            )
            for a in range(some)
        ],
        0,
    )
    bias = jnp.concatenate(
        [jnp.sum(bias_ref[a, 0, 0:3, :].astype(F32), 0, keepdims=True) for a in range(some)], 1
    )
    pre = mm(x_ref[...], widen) + bias
    cumulative, slope = gelu_parts(pre)
    hidden = (pre * cumulative).astype(BF16)
    grad_pre = (mm(g_ref[...], narrow, NT) * (cumulative + slope)).astype(BF16)
    hidden_ref[0] = hidden
    pre_ref[0] = grad_pre
    bias_grad_ref[0] = jnp.sum(grad_pre.astype(F32), 0, keepdims=True)
    out = mm(hidden, narrow)
    dx = mm(grad_pre, widen, NT)

    @pl.when(step == 0)
    def _():
        out_s[...] = out
        dx_s[...] = dx

    @pl.when(step > 0)
    def _():
        out_s[...] += out
        dx_s[...] += dx

    @pl.when(step == pl.num_programs(0) - 1)
    def _():
        out_ref[...] = out_s[...].astype(out_ref.dtype)
        dx_ref[...] = dx_s[...].astype(dx_ref.dtype)


def feed(normed, grad, rest, bias_at, some, dtype):
    shards, count, _, tile = rest.shape
    rows, width = normed.shape
    depth = width // count
    parts = width // tile
    steps = shards // some
    unit_spec = pl.BlockSpec((1, rows, some * tile), lambda m: (m, 0, 0))
    return pl.pallas_call(
        functools.partial(feed_kernel, parts),
        grid=(steps,),
        in_specs=[
            whole((rows, width)),
            whole((rows, width)),
            pl.BlockSpec((some, count, depth, tile), lambda m: (m, 0, 0, 0)),
            pl.BlockSpec((some, count, depth, tile), lambda m: (m, 0, 1, 0)),
            pl.BlockSpec((some, 1, 16, tile), lambda m: (m, 0, bias_at // 16, 0)),
        ],
        out_specs=[
            whole((rows, width)),
            whole((rows, width)),
            unit_spec,
            unit_spec,
            pl.BlockSpec((1, 1, some * tile), lambda m: (m, 0, 0)),
        ],
        out_shape=[
            jax.ShapeDtypeStruct((rows, width), dtype),
            jax.ShapeDtypeStruct((rows, width), dtype),
            jax.ShapeDtypeStruct((steps, rows, some * tile), BF16),
            jax.ShapeDtypeStruct((steps, rows, some * tile), BF16),
            jax.ShapeDtypeStruct((steps, 1, some * tile), F32),
        ],
        scratch_shapes=[pltpu.VMEM((rows, width), F32), pltpu.VMEM((rows, width), F32)],
        compiler_params=params(),
        cost_estimate=cost(8 * shards * rows * width * tile, rest.size * 2 + rows * width * 28, rows * shards * tile),
    )(normed, grad, rest, rest, rest)


def feed_grads_kernel(*refs):
    out_ref = refs[-1]
    some, count, both, width = out_ref.shape
    piece = both // 2
    widen = narrow = 0.0
    for at in range(0, len(refs) - 1, 4):
        x_ref, g_ref, hidden_ref, pre_ref = refs[at : at + 4]
        widen += mm(pre_ref[0], x_ref[...], TN)
        narrow += mm(hidden_ref[0], g_ref[...], TN)
    out_ref[:, :, :piece, :] = widen.astype(BF16).reshape(some, count, piece, width)
    out_ref[:, :, piece:, :] = narrow.astype(BF16).reshape(some, count, piece, width)


def feed_grads(feed_parts, count, some, extra):
    steps, _, tiles = feed_parts[0][2].shape
    width = feed_parts[0][0].shape[1]
    both = 2 * tiles // some // count
    specs, rows_all = [], 0
    for part in feed_parts:
        rows = part[0].shape[0]
        rows_all += rows
        unit_spec = pl.BlockSpec((1, rows, tiles), lambda m: (m, 0, 0))
        specs += [whole((rows, width)), whole((rows, width)), unit_spec, unit_spec]
    return pl.pallas_call(
        feed_grads_kernel,
        grid=(steps,),
        in_specs=specs,
        out_specs=pl.BlockSpec((some, count, both, width), lambda m: (m, 0, 0, 0)),
        out_shape=jax.ShapeDtypeStruct((steps * some, count, both + extra, width), BF16),
        compiler_params=params(),
        cost_estimate=cost(4 * steps * rows_all * width * tiles, steps * rows_all * tiles * 4 + steps * tiles * width * 4),
    )(*[array for part in feed_parts for array in part])


def merge_kernel(shards, slots, place_ref, got_ref, w_ref, start_ref, vec_ref, ctx_ref, middle_ref, normed_ref):
    b = pl.program_id(0)
    wide = got_ref.shape[-1]
    for p in range(shards):
        ctx_ref[:, p * wide : (p + 1) * wide] = got_ref[place_ref[b * shards + p]]
    middle = start_ref[...] + mm(ctx_ref[...], w_ref[...]) + vec_ref[0:1, :]
    middle_ref[...] = middle
    normal, _ = norm_parts(middle)
    normed_ref[...] = (normal * vec_ref[1:2, :] + vec_ref[2:3, :]).astype(BF16)


def merge(got, weight, start, vectors, places, slots):
    count, block, wide = got.shape
    rows, width = start.shape
    shards = width // wide
    row_spec = pl.BlockSpec((block, width), lambda b, t: (b, 0))
    return pl.pallas_call(
        functools.partial(merge_kernel, shards, slots),
        grid_spec=pltpu.PrefetchScalarGridSpec(
            num_scalar_prefetch=1,
            grid=(slots,),
            in_specs=[
                pl.BlockSpec(got.shape, lambda b, t: (0, 0, 0)),
                pl.BlockSpec(weight.shape, lambda b, t: (0, 0)),
                row_spec,
                pl.BlockSpec(vectors.shape, lambda b, t: (0, 0)),
            ],
            out_specs=[row_spec, row_spec, row_spec],
        ),
        out_shape=[
            jax.ShapeDtypeStruct((rows, width), BF16),
            jax.ShapeDtypeStruct((rows, width), F32),
            jax.ShapeDtypeStruct((rows, width), BF16),
        ],
        compiler_params=params(),
        cost_estimate=cost(2 * rows * width * width, rows * width * 20),
    )(places, got, weight, start, vectors)


def merge_back_kernel(shards, count, shard_ref, g_ref, w_ref, out_ref, dctx_s):
    wide = out_ref.shape[-1]
    grad = g_ref[...]
    for p in range(shards):
        dctx_s[p] = mm(grad, w_ref[p * wide : (p + 1) * wide, :], NT).astype(BF16)
    for i in range(count):
        out_ref[i] = dctx_s[shard_ref[i]]


def merge_back(grad, weight, shard_of, wide):
    rows, width = grad.shape
    shards = width // wide
    count = shard_of.shape[0]
    return pl.pallas_call(
        functools.partial(merge_back_kernel, shards, count),
        grid_spec=pltpu.PrefetchScalarGridSpec(
            num_scalar_prefetch=1,
            grid=(1,),
            in_specs=[
                pl.BlockSpec((rows, width), lambda b, t: (0, 0)),
                pl.BlockSpec((width, width), lambda b, t: (0, 0)),
            ],
            out_specs=pl.BlockSpec((count, rows, wide), lambda b, t: (0, 0, 0)),
            scratch_shapes=[pltpu.VMEM((shards, rows, wide), BF16)],
        ),
        out_shape=jax.ShapeDtypeStruct((count, rows, wide), BF16),
        compiler_params=params(),
        cost_estimate=cost(2 * rows * width * width, rows * width * 8),
    )(shard_of, grad, weight)


def norm_parts(value):
    mean = jnp.mean(value, -1, keepdims=True)
    centred = value - mean
    scale = lax.rsqrt(jnp.mean(centred * centred, -1, keepdims=True) + EPSILON)
    return centred * scale, scale


def norm_back(normal, scale, gain, grad):
    grad_x = grad * gain
    mean = jnp.mean(grad_x, -1, keepdims=True)
    along = jnp.mean(grad_x * normal, -1, keepdims=True)
    return (
        (grad_x - mean - normal * along) * scale,
        jnp.sum(grad * normal, 0),
        jnp.sum(grad, 0),
    )


def share_of(array, at, count):
    share = array.shape[0] // count
    return lax.dynamic_slice_in_dim(array, at * share, share, 0)


def on_device(
    tokens,
    cotangent,
    group_items,
    dataset_ids,
    lead_hours,
    set_weights,
    lead_weight,
    lead_shift,
    norm_one_gain,
    norm_one_shift,
    heads_weight,
    heads_bias,
    merge_weight,
    merge_bias,
    norm_two_gain,
    norm_two_shift,
    widen_weight,
    widen_bias,
    narrow_weight,
    narrow_bias,
):
    shards = lax.axis_size("mp")
    copies = lax.axis_size("dp")
    rows_here, width = tokens.shape
    group_rows = rows_here * shards
    slots = dataset_ids.shape[0]
    length = group_rows // slots
    block = rows_here // slots
    cols = heads_weight.shape[1]
    heads_here = cols // (3 * HEAD_DIM)
    wide = heads_here * HEAD_DIM
    tile = widen_weight.shape[1] // 2
    parts = width // tile
    count = copies // 2
    some = 4
    dp_at = lax.axis_index("dp")
    mp_at = lax.axis_index("mp")
    both = ("dp", "mp")

    def attention_device(group, k):
        return (group // 2 * 2 + k % 2) * shards + k // 2 * 2 + group % 2

    def row_device(group, k):
        return group * shards + k

    groups = range(copies)
    spots = range(shards)

    def meet(k_rows, k_unit):
        return any(
            (slots * k_rows + b) // shards == (slots * k_unit + j) // shards
            for b in range(slots)
            for j in range(slots)
        )

    core_swap = [(g, g + 1 - g % 2 * 2) for g in groups]
    half_swap = [(g, g ^ 2) for g in groups]
    half_at = dp_at // 2 % 2
    piece_at = dp_at // 4 * 2 + dp_at % 2
    plane = [[k * copies + g for k in spots for g in groups if g // 2 % 2 == h] for h in range(2)]
    row_swap = [(k, k + 1 - k % 2 * 2) for k in spots]
    reach = max(abs(a // 2 - b // 2) for a in spots for b in spots if meet(a, b))
    classes = []
    for s in sorted(range(1 - shards, shards), key=abs):
        pairs = [(k, k + s) for k in spots if 0 <= k + s < shards and meet(k + s, k)]
        for known in classes:
            if not any(a == c or b == d for a, b in pairs for c, d in known):
                known += pairs
                break
        else:
            if pairs:
                classes.append(pairs)
    color = [[0] * shards for _ in spots]
    senders = [[0] * shards for _ in classes]
    for i, pairs in enumerate(classes):
        for unit, rows in pairs:
            color[unit][rows] = i
            senders[i][rows] = unit
    color = jnp.asarray(color, jnp.int32)
    senders = jnp.asarray(senders, jnp.int32)

    def extents(pairs):
        ranges = []
        for unit, rows in pairs:
            shared = [
                (j, b)
                for j in range(slots)
                for b in range(slots)
                if (slots * rows + b) // shards == (slots * unit + j) // shards
            ]
            ranges.append([(min(part), max(part) + 1) for part in zip(*shared)])
        sizes = [max(r[at][1] - r[at][0] for r in ranges) for at in range(2)]
        unit_starts = [[0] * shards for _ in range(2)]
        row_starts = [[0] * shards for _ in range(2)]
        for (unit, rows), r in zip(pairs, ranges):
            for at in range(2):
                unit_starts[at][unit] = row_starts[at][rows] = min(r[at][0], slots - sizes[at])
        return sizes, unit_starts, row_starts

    def exchange(array, to_rows):
        got = []
        for i, pairs in enumerate(classes):
            sizes, unit_starts, row_starts = extents(pairs)
            ends = [(attention_device(g, unit), row_device(g, rows)) for g in groups for unit, rows in pairs]
            ends = ends if to_rows else back(ends)
            message = array[i]
            if sizes == [slots, slots]:
                got.append(lax.ppermute(message, both, ends))
                continue
            at_unit = [jnp.asarray(part, jnp.int32)[k_here] for part in unit_starts]
            at_rows = [jnp.asarray(part, jnp.int32)[mp_at] for part in row_starts]
            at_from, at_to = (at_unit, at_rows) if to_rows else (at_rows, at_unit)
            some_part = lax.dynamic_slice(message, (*at_from, 0, 0), (*sizes, *message.shape[2:]))
            some_part = lax.ppermute(some_part, both, ends)
            got.append((some_part, at_to))
        return got

    def together(got, shape):
        whole_ones = [
            lax.dynamic_update_slice(jnp.zeros(shape, BF16), part[0], (*part[1], 0, 0))
            if isinstance(part, tuple)
            else part
            for part in got
        ]
        return jnp.stack(whole_ones).reshape(-1, *shape[2:])

    def far(step):
        return [
            (attention_device(g, k), row_device(g, k + 2 * step))
            for g in groups
            for k in spots
            if 0 <= k + 2 * step < shards and any(meet(k + 2 * step, k // 2 * 2 + b) for b in range(2))
        ]

    def back(pairs):
        return [(b, a) for a, b in pairs]

    steps = range(-reach, reach + 1)

    k_here = mp_at // 2 * 2 + dp_at % 2
    unit_ids = slots * k_here + jnp.arange(slots, dtype=jnp.int32)
    unit_items = unit_ids // shards
    unit_blocks = unit_items[:, None] * shards + jnp.arange(shards, dtype=jnp.int32)[None, :]
    block_spots = unit_blocks // slots
    table = jnp.stack(
        [
            (block_spots + dp_at) % 2,
            (block_spots // 2 - mp_at // 2 + reach) * slots + unit_blocks % slots,
        ],
        2,
    )
    table = jnp.concatenate([table.reshape(-1), unit_items, unit_ids % shards]).astype(jnp.int32)
    counting = jnp.arange(slots, dtype=jnp.int32)
    unit_places = (
        (color[k_here, block_spots] * slots + counting[:, None]) * slots + unit_blocks % slots
    ).reshape(-1)
    row_units = ((slots * mp_at + counting) // shards * shards)[:, None] + jnp.arange(
        shards, dtype=jnp.int32
    )[None, :]
    row_places = (
        (color[row_units // slots, mp_at] * slots + row_units % slots) * slots + counting[:, None]
    ).reshape(-1)
    wanted = ((slots * senders[:, mp_at][:, None] + counting[None, :]) % shards).reshape(-1)

    def weight_pairs(j):
        return [
            (g * shards + (slots * k + j) % shards, attention_device(g, k)) for g in groups for k in spots
        ]

    def exact_rows(vector, pad):
        high = vector.astype(BF16)
        left = vector - high.astype(F32)
        middle = left.astype(BF16)
        low = (left - middle.astype(F32)).astype(BF16)
        return jnp.pad(jnp.stack([high, middle, low]), ((0, pad - 3), (0, 0)))

    bias_heads = heads_bias.reshape(heads_here, 2, HEAD_DIM)
    full_bias = jnp.stack(
        [bias_heads[:, 0], jnp.zeros_like(bias_heads[:, 0]), bias_heads[:, 1]], 1
    ).reshape(-1)
    heads_rows = jnp.concatenate([heads_weight, exact_rows(full_bias, 16 * count)], 0)
    heads_piece = share_of(heads_rows, piece_at, count)
    heads_piece, tokens = lax.optimization_barrier((heads_piece, tokens))
    heads_all = lax.all_gather(heads_piece, BOTH, axis=0, tiled=True, axis_index_groups=plane)
    heads_all = heads_all.reshape(shards, -1, cols)

    row_ids = mp_at * rows_here + jnp.arange(rows_here, dtype=jnp.int32)
    slot_ids = jnp.arange(slots, dtype=jnp.int32)
    slot_table = ((row_ids // length)[:, None] == slot_ids[None, :]).astype(F32)
    lead_scaled = jnp.sum(slot_table * (lead_hours.astype(F32) / 100.0)[None, :], 1)
    live = (slot_ids < group_items[0]).astype(F32)
    set_ids = jnp.arange(set_weights.shape[0], dtype=jnp.int32)
    set_match = (dataset_ids[:, None] == set_ids[None, :]).astype(F32)
    item_weight = live * jnp.sum(set_match * set_weights[None, :], 1)
    row_weight = jnp.sum(slot_table * item_weight[None, :], 1)

    start_state = tokens + lead_scaled[:, None] * lead_weight + lead_shift
    first_normal, first_scale = norm_parts(start_state)
    normed_one = (first_normal * norm_one_gain + norm_one_shift).astype(BF16)

    def fold(part):
        return jnp.concatenate(jnp.split(part, parts, 1), 0)

    rest = jnp.concatenate(
        [
            share_of(lax.dynamic_slice_in_dim(widen_weight, half_at * tile, tile, 1), piece_at, count),
            fold(share_of(share_of(narrow_weight, half_at, 2), piece_at, count)),
            fold(share_of(merge_weight, piece_at, count)),
            exact_rows(share_of(widen_bias, half_at, 2), 16),
        ],
        0,
    )
    merge_rows = merge_weight.shape[0] // count
    merge_at = 2 * (width // count)
    bias_at = merge_at + merge_rows * parts

    own = jnp.stack([lax.ppermute(normed_one, both, back(far(o))) for o in steps])
    grad_out = cotangent * row_weight[:, None]
    grad_low = grad_out.astype(BF16)
    own, rest, grad_low, live_items = lax.optimization_barrier((own, rest, grad_low, group_items))
    item_total = lax.psum(live_items.astype(F32)[0], "dp")
    rest = lax.all_gather(rest, BOTH, axis=0, tiled=True, axis_index_groups=plane)
    rest = rest.reshape(shards, count, -1, tile)
    their_grad = lax.ppermute(grad_low, "dp", half_swap)
    other = lax.ppermute(own, "dp", core_swap)
    other, item_total = lax.optimization_barrier((other, item_total))
    pieces = [part.reshape(-1, block, width) for part in (own, other)]

    packed = project(pieces, heads_all, table, length, slots)
    messages = len(classes) * slots * slots
    message = (slots, slots, block, wide)
    context, lse = attend(packed, heads_here, block, unit_places, messages)
    context_got = together(exchange(context.reshape(-1, *message), True), message)
    merge_all = rest[:, :, merge_at:bias_at, :].reshape(shards, count, parts, merge_rows, tile)
    merge_all = merge_all.transpose(0, 1, 3, 2, 4).reshape(width, width)
    merge_vectors = jnp.pad(jnp.stack([merge_bias, norm_two_gain, norm_two_shift]), ((0, 5), (0, 0)))
    context_rows, middle, normed_two = merge(
        context_got, merge_all, start_state, merge_vectors, row_places, slots
    )
    second_normal, second_scale = norm_parts(middle)

    narrow_bias_grad = jnp.sum(grad_low.astype(F32), 0)
    chunk = rows_here // 2
    chunks = [slice(0, chunk), slice(chunk, rows_here)]
    their_normed = [lax.ppermute(normed_two[rows], "dp", half_swap) for rows in chunks]
    fed, grad_norm_two, hidden, grad_pre, widen_bias_grad = feed(
        normed_two, grad_low, rest, bias_at, some, F32
    )
    feed_parts = [(normed_two, grad_low, hidden, grad_pre)]
    their_fed, their_dx = [], []
    for i, rows in enumerate(chunks):
        their_normed[i], fed = lax.optimization_barrier((their_normed[i], fed))
        their = (their_normed[i], their_grad[rows])
        part_fed, part_dx, hidden, grad_pre, part_bias = feed(*their, rest, bias_at, some, BF16)
        feed_parts.append(their + (hidden, grad_pre))
        widen_bias_grad += part_bias
        their_fed.append(part_fed)
        their_dx.append(lax.ppermute(part_dx, "dp", half_swap))
        fed = lax.optimization_barrier((fed, part_dx))[0]
    grads_one = feed_grads(feed_parts, count, some, merge_weight.shape[0] // copies)
    their_dx[-1], grads_one, *their_fed = lax.optimization_barrier((their_dx[-1], grads_one, *their_fed))
    grad_norm_two = grad_norm_two + jnp.concatenate(their_dx).astype(F32)
    their_fed = lax.ppermute(jnp.concatenate(their_fed), "dp", half_swap)
    widen_bias_grad = widen_bias_grad.reshape(shards, 1, tile)
    widen_bias_grad = jnp.where(
        jnp.arange(2, dtype=jnp.int32)[None, :, None] == half_at, widen_bias_grad, 0.0
    )
    grad_mid_norm, norm_two_gain_grad, norm_two_shift_grad = norm_back(
        second_normal, second_scale, norm_two_gain, grad_norm_two
    )
    grad_middle = grad_out + grad_mid_norm
    grad_mid_low = grad_middle.astype(BF16)
    merge_bias_grad = jnp.sum(grad_mid_low.astype(F32), 0)
    grad_context = merge_back(grad_mid_low, merge_all, wanted, wide)
    grad_context = exchange(grad_context.reshape(-1, *message), False)
    grad_context = together(grad_context, message)
    merge_weight_grad = mm(context_rows, grad_mid_low, TN).astype(BF16)
    merge_weight_grad = merge_weight_grad.reshape(shards, copies // 4, 2, 2, -1, width)
    kept = lax.dynamic_index_in_dim(merge_weight_grad, half_at, 2, False)
    sent = lax.dynamic_index_in_dim(merge_weight_grad, 1 - half_at, 2, False)
    kept = kept.astype(F32) + lax.ppermute(sent, "dp", half_swap).astype(F32)
    grads_one = grads_one.at[:, :, 2 * (tile // count) :].set(
        kept.astype(BF16).reshape(shards, count, -1, width)
    )
    grads_one = lax.psum_scatter(
        grads_one.reshape(-1, width), BOTH, scatter_dimension=0, tiled=True, axis_index_groups=plane
    )
    grad_packed, unit_sums = attend_back(
        packed, context, grad_context, lse, heads_here, block, unit_places
    )
    grad_packed, their_fed = lax.optimization_barrier((grad_packed, their_fed))
    activations = middle + fed + their_fed.astype(F32) + narrow_bias
    unit_grads = weight_back(pieces, grad_packed, table)
    heads_parts = [lax.ppermute(unit_grads[j], both, back(weight_pairs(j))) for j in range(slots)]
    grad_packed, unit_grads = lax.optimization_barrier((grad_packed, unit_grads))
    own_dx, other_dx = rows_back(grad_packed, heads_all, table, block, 2, len(steps) * slots, width)

    other_dx = lax.ppermute(other_dx, "dp", core_swap)
    other_dx, *heads_parts = lax.optimization_barrier((other_dx, *heads_parts))
    other_dx = other_dx.reshape(-1, rows_here, width)
    own_dx = own_dx.reshape(-1, rows_here, width)
    pair_dx = [(own_dx[i].astype(F32) + other_dx[i].astype(F32)).astype(BF16) for i in range(len(steps))]
    grad_norm_one = [lax.ppermute(pair_dx[i], both, far(o)) for i, o in enumerate(steps)]

    heads_total = sum(part.astype(F32) for part in heads_parts).astype(BF16)
    for bit in range((copies - 1).bit_length()):
        over = lax.ppermute(heads_total, "dp", [(g, g ^ 1 << bit) for g in groups])
        heads_total = (heads_total.astype(F32) + over.astype(F32)).astype(BF16)
    grad_norm_one[-1], heads_total = lax.optimization_barrier((grad_norm_one[-1], heads_total))
    grad_norm_one = sum(part.astype(F32) for part in grad_norm_one)
    heads_bias_grad = jnp.sum(
        jnp.where(
            (unit_ids % shards)[:, None, None] == jnp.arange(shards, dtype=jnp.int32)[None, :, None],
            unit_sums,
            0.0,
        ),
        0,
    )

    grad_start_norm, norm_one_gain_grad, norm_one_shift_grad = norm_back(
        first_normal, first_scale, norm_one_gain, grad_norm_one
    )
    grad_start = grad_middle + grad_start_norm
    lead_weight_grad = jnp.sum(grad_start * lead_scaled[:, None], 0)
    lead_shift_grad = jnp.sum(grad_start, 0)
    vectors = (
        lead_weight_grad,
        lead_shift_grad,
        norm_one_gain_grad,
        norm_one_shift_grad,
        merge_bias_grad,
        norm_two_gain_grad,
        norm_two_shift_grad,
        narrow_bias_grad,
    )
    vectors = jnp.concatenate(
        [jnp.stack(vectors).reshape(-1), widen_bias_grad.reshape(-1), heads_bias_grad.reshape(-1)]
    )
    hops = [
        (axis, [(i, i ^ 1 << bit) for i in range(size)])
        for axis, size in (("mp", shards), ("dp", copies))
        for bit in range((size - 1).bit_length())
    ]
    for axis, pairs in hops:
        vectors += lax.ppermute(vectors, axis, pairs)
    vectors /= item_total
    heads_total = heads_total.astype(F32)
    shared = vectors[: 8 * width].reshape(8, width)
    place = lax.axis_index("mp")
    widen_bias_total = lax.dynamic_slice_in_dim(vectors, 8 * width + place * 2 * tile, 2 * tile, 0)
    heads_bias_total = lax.dynamic_slice_in_dim(
        vectors, 8 * width + shards * 2 * tile + place * cols, cols, 0
    ).reshape(heads_here, 3, HEAD_DIM)
    heads_bias_total = jnp.stack([heads_bias_total[:, 0], heads_bias_total[:, 2]], 1).reshape(-1)

    grads_one = lax.all_gather(grads_one, "dp", axis=0, tiled=True).astype(F32) / item_total
    piece = tile // count
    grads_one = grads_one.reshape(copies // 4, 2, 2, -1, width).transpose(1, 0, 2, 3, 4)
    widen_total = grads_one[:, :, :, :piece].reshape(2 * tile, width).T
    narrow_total = grads_one[:, :, :, piece : 2 * piece].reshape(2 * tile, width)
    merge_total = grads_one[:, :, :, 2 * piece :].transpose(1, 0, 2, 3, 4).reshape(-1, width)
    heads_total = heads_total.T / item_total
    return (
        activations,
        grad_start / item_total,
        shared[0],
        shared[1],
        shared[2],
        shared[3],
        heads_total,
        heads_bias_total,
        merge_total,
        shared[4],
        shared[5],
        shared[6],
        widen_total,
        widen_bias_total,
        narrow_total,
        shared[7],
    )


def solution(mesh):
    return jax.shard_map(
        on_device,
        mesh=mesh,
        in_specs=(
            P(("dp", "mp"), None),
            P(("dp", "mp"), None),
            P("dp"),
            P("dp"),
            P("dp"),
            P(),
            P(),
            P(),
            P(),
            P(),
            P(None, "mp"),
            P("mp"),
            P("mp", None),
            P(),
            P(),
            P(),
            P(None, "mp"),
            P("mp"),
            P("mp", None),
            P(),
        ),
        out_specs=(
            P(("dp", "mp"), None),
            P(("dp", "mp"), None),
            P(),
            P(),
            P(),
            P(),
            P(None, "mp"),
            P("mp"),
            P("mp", None),
            P(),
            P(),
            P(),
            P(None, "mp"),
            P("mp"),
            P("mp", None),
            P(),
        ),
        check_vma=False,
    )
```
